32 devices in a mesh: groups: 2 (over y), row: 4 (over z), col: 4 (over x, core).
Axes of the slice: x: 2, y: 2, z: 4, core: 2. Of those that a mesh axis runs over, the one named last changes fastest.
Arguments:
- pair_map: bfloat16 [320, 160, 128], P(('groups', 'row'), 'col'), parts along dimension 0, may hold values from -6 to 6
- token_mask: int32 [320], P('groups'), parts along dimension 0, may hold values 0 or 1
- in_gain: float32 [2, 128], replicated, may hold values from 0.5 to 1.5
- proj_weights: bfloat16 [2, 4, 128, 128], replicated, may hold values from -0.5 to 0.5
- gate_weight: bfloat16 [2, 128, 128], replicated, may hold values from -0.5 to 0.5
- out_gain: float32 [2, 128], replicated, may hold values from 0.5 to 1.5
- out_weight: bfloat16 [2, 128, 128], replicated, may hold values from -0.5 to 0.5
Outputs:
- updated_pair: bfloat16 [320, 160, 128], P(('groups', 'row'), 'col'), parts along dimension 0
The draws below stay inside these ranges and needn't reach their ends.
There are 2 independent parts, one for each index of `groups`. The reference program is written for one: setup_inputs(seed, part) draws one part's arguments, and reference() takes and returns one part's arrays. A program takes and returns all parts, laid end to end along the dimension named above; an argument that names none is the same for every part. Nothing has to cross between parts.
All inputs are finite; a program needn't handle non-finite values.
Results may differ from the reference program's by a relative error of at most 0.015.
Values may be sent and summed in bfloat16 or wider, within the bound.
No kernel may reach another device: no remote copies, remote signals or barrier semaphores. Data moves between devices by JAX's collectives and lax.ppermute only.
A program may use at most 128 MiB of HBM per device.

```python
import jax
import jax.numpy as jnp
from jax import lax

C = 128
HID = 128
TOKENS = 160
N_ROW = 4
N_COL = 4


def place_ends(result, stream_key, smallest, largest):
    extent = result.shape
    index_at = [jax.random.randint(jax.random.fold_in(stream_key, axis), (), 0, extent[axis]) for axis in range(len(extent))]
    result = result.at[tuple(index_at)].set(smallest)
    longest = extent.index(max(extent))
    index_at[longest] = (index_at[longest] + 1) % extent[longest]
    return result.at[tuple(index_at)].set(largest)


def level_of(key, extent, shards, low, largest):
    loudness, own = 1.0, jax.random.fold_in(key, 6)
    for dim, blocks in shards:
        heights = jnp.exp(jax.random.uniform(jax.random.fold_in(own, dim), (blocks,), jnp.float32, low / len(shards), largest / len(shards)))
        loudness = loudness * jnp.repeat(heights, extent[dim] // blocks).reshape([-1 if axis == dim else 1 for axis in range(len(extent))])
    return loudness


def noise(stream_key, shape, spread, bound, cuts=(), dtype=jnp.bfloat16):
    result = jax.random.normal(stream_key, shape, jnp.float32) * spread
    if len(cuts) > 0:
        result = level_of(stream_key, shape, cuts, -0.22, 0.18) * result
    return jnp.clip(result, min=-bound, max=bound).astype(dtype)


def setup_inputs(seed: int = 0, part: int = 0) -> dict:
    arg_keys = jax.random.split(jax.random.key(seed), 8)
    part_splits = jax.random.split(jax.random.fold_in(arg_keys[7], part), 8)
    pair_map = noise(part_splits[0], (TOKENS, TOKENS, C), 1.0, 6.0, ((0, 4), (1, 4)))
    token_mask = place_ends((jax.random.randint(part_splits[1], (TOKENS,), 0, 8) < 7).astype(jnp.int32), jax.random.fold_in(part_splits[1], 1), 0, 1)
    in_gain = jnp.clip(1.0 + 0.1 * jax.random.normal(arg_keys[2], (2, C), jnp.float32), 0.5, 1.5)
    proj_weights = noise(arg_keys[3], (2, 4, C, HID), C ** -0.5, 0.5)
    gate_weight = noise(arg_keys[4], (2, C, C), C ** -0.5, 0.5)
    out_gain = jnp.clip(1.0 + 0.1 * jax.random.normal(arg_keys[5], (2, HID), jnp.float32), 0.5, 1.5)
    out_weight = noise(arg_keys[6], (2, HID, C), HID ** -0.5, 0.5)
    return {"pair_map": pair_map, "token_mask": token_mask, "in_gain": in_gain, "proj_weights": proj_weights, "gate_weight": gate_weight, "out_gain": out_gain, "out_weight": out_weight}


EPSILON = 1e-05

def layer_norm(values, gain_vec):
    mean_val = lax.optimization_barrier(jnp.mean(values, axis=-1, keepdims=True))
    centered = values - mean_val
    variance = lax.optimization_barrier(jnp.mean(centered * centered, axis=-1, keepdims=True))
    return centered * jax.lax.rsqrt(variance + EPSILON) * gain_vec

def project_side(pair_tile, pair_valid, layer_index, in_gain, proj_weights, gate_weight):
    normed = layer_norm(pair_tile.astype(jnp.float32), in_gain[layer_index]).astype(jnp.bfloat16)
    outputs = [jnp.dot(normed, proj_weights[layer_index, slot], preferred_element_type=jnp.float32) for slot in range(4)]
    weight_mask = pair_valid[..., None]
    left_side = (jax.nn.sigmoid(outputs[1]) * outputs[0] * weight_mask).astype(jnp.bfloat16)
    right_side = (jax.nn.sigmoid(outputs[3]) * outputs[2] * weight_mask).astype(jnp.bfloat16)
    gating = jax.nn.sigmoid(jnp.dot(normed, gate_weight[layer_index], preferred_element_type=jnp.float32))
    return (left_side, right_side, gating)

def finish(pair_tile, mixed_sum, gating, layer_index, out_gain, out_weight):
    normed = layer_norm(mixed_sum, out_gain[layer_index]).astype(jnp.bfloat16)
    update = jnp.dot(normed, out_weight[layer_index], preferred_element_type=jnp.float32)
    return (pair_tile.astype(jnp.float32) + gating * update).astype(jnp.bfloat16)

def blockwise(left_blocks, right_blocks, form, out_shape):

    def step(total, pieces):
        part = jnp.einsum(form, pieces[0].astype(jnp.float32), pieces[1].astype(jnp.float32))
        part = lax.optimization_barrier(part.astype(jnp.bfloat16))
        return (total + part.astype(jnp.float32), None)
    init = jnp.zeros(out_shape, jnp.float32)
    total, unused = lax.scan(step, init, (left_blocks, right_blocks))
    return total

def reference(pair_map, token_mask, in_gain, proj_weights, gate_weight, out_gain, out_weight):
    count = pair_map.shape[0]
    width = proj_weights.shape[3]
    valid = token_mask.astype(jnp.float32)
    pair_valid = valid[:, None] * valid[None, :]
    left_side, right_side, gating = project_side(pair_map, pair_valid, 0, in_gain, proj_weights, gate_weight)
    col_block = count // N_COL
    left_blocks = jnp.moveaxis(left_side.reshape(count, N_COL, col_block, width), 1, 0)
    right_blocks = jnp.moveaxis(right_side.reshape(count, N_COL, col_block, width), 1, 0)
    mixed = blockwise(left_blocks, right_blocks, 'ikc,jkc->ijc', (count, count, width))
    after_out = finish(pair_map, mixed, gating, 0, out_gain, out_weight)
    left_side, right_side, gating = project_side(after_out, pair_valid, 1, in_gain, proj_weights, gate_weight)
    row_block = count // N_ROW
    left_blocks = left_side.reshape(N_ROW, row_block, count, width)
    right_blocks = right_side.reshape(N_ROW, row_block, count, width)
    mixed = blockwise(left_blocks, right_blocks, 'kic,kjc->ijc', (count, count, width))
    return finish(after_out, mixed, gating, 1, out_gain, out_weight)
```

```python
import functools

import jax
import jax.numpy as jnp
from jax import lax
from jax.experimental import pallas as pl
from jax.experimental.pallas import tpu as pltpu
from jax.sharding import PartitionSpec as P

EPSILON = 1e-05
LANES = 128
F32 = jnp.float32
BF16 = jnp.bfloat16


def layer_norm(values, gain_vec):
    mean_val = jnp.mean(values, axis=-1, keepdims=True)
    centered = values - mean_val
    variance = jnp.mean(centered * centered, axis=-1, keepdims=True)
    return centered * jax.lax.rsqrt(variance + EPSILON) * gain_vec


def project_side(pair_tile, pair_valid, layer_index, in_gain, proj_weights, gate_weight):
    normed = layer_norm(pair_tile.astype(F32), in_gain[layer_index]).astype(BF16)
    outputs = [
        jnp.dot(normed, proj_weights[layer_index, slot], preferred_element_type=F32)
        for slot in range(4)
    ]
    weight_mask = pair_valid[..., None]
    left_side = (jax.nn.sigmoid(outputs[1]) * outputs[0] * weight_mask).astype(BF16)
    right_side = (jax.nn.sigmoid(outputs[3]) * outputs[2] * weight_mask).astype(BF16)
    gating = jax.nn.sigmoid(jnp.dot(normed, gate_weight[layer_index], preferred_element_type=F32))
    return (left_side, right_side, gating)


def finish(pair_tile, mixed_sum, gating, layer_index, out_gain, out_weight):
    normed = layer_norm(mixed_sum, out_gain[layer_index]).astype(BF16)
    update = jnp.dot(normed, out_weight[layer_index], preferred_element_type=F32)
    return (pair_tile.astype(F32) + gating * update).astype(BF16)


def pair_mask(token_mask, tile_rows, row_begin, tile_cols, col_begin):
    valid = token_mask.astype(F32)
    row_valid = lax.dynamic_slice_in_dim(valid, row_begin, tile_rows, 0)
    col_valid = lax.dynamic_slice_in_dim(valid, col_begin, tile_cols, 0)
    return row_valid[:, None] * col_valid[None, :]


def gather_body(pair_map, token_mask, in_gain, proj_weights, gate_weight, out_gain, out_weight):
    tile_rows, tile_cols = pair_map.shape[:2]
    pair_valid = pair_mask(
        token_mask,
        tile_rows,
        lax.axis_index("row") * tile_rows,
        tile_cols,
        lax.axis_index("col") * tile_cols,
    )
    left_side, right_side, gating = project_side(
        pair_map, pair_valid, 0, in_gain, proj_weights, gate_weight
    )
    block = lax.all_gather(right_side, "row", axis=0, tiled=True)
    summed = lax.psum_scatter(
        jnp.einsum("jkc,ikc->jic", block, left_side, preferred_element_type=F32).astype(BF16),
        "col",
        scatter_dimension=0,
        tiled=True,
    ).astype(F32)
    mixed = jnp.transpose(summed, (1, 0, 2))
    after_out = finish(pair_map, mixed, gating, 0, out_gain, out_weight)
    left_side, right_side, gating = project_side(
        after_out, pair_valid, 1, in_gain, proj_weights, gate_weight
    )
    block = lax.all_gather(left_side, "col", axis=1, tiled=True)
    mixed = lax.psum_scatter(
        jnp.einsum("kic,kjc->ijc", block, right_side, preferred_element_type=F32).astype(BF16),
        "row",
        scatter_dimension=0,
        tiled=True,
    ).astype(F32)
    return finish(after_out, mixed, gating, 1, out_gain, out_weight)


NEAR = 4


class Place:
    def __init__(self):
        z = lax.axis_index("row")
        col = lax.axis_index("col")
        self.z = z
        self.x = lax.div(col, 2)
        self.core = lax.rem(col, 2)
        self.half = lax.div(z, 2)
        self.group = lax.rem(z, 2) * 2 + self.x

    def channels(self, d, ch, other=False):
        core = 1 - self.core if other else self.core
        begin = jnp.bitwise_xor(self.group, d) * (2 * ch) + core * ch
        return pl.ds(pl.multiple_of(begin, ch), ch)


def lane_of(rows):
    return lax.broadcasted_iota(jnp.int32, (rows, LANES), 1)


def take_piece(value, index, width, lane):
    tile, offset = divmod(index * width, LANES)
    part = value[:, tile * LANES : (tile + 1) * LANES]
    if offset:
        part = pltpu.roll(part, LANES - offset, 1)
    if offset + width > LANES:
        after = value[:, (tile + 1) * LANES : (tile + 2) * LANES]
        part = jnp.where(lane < LANES - offset, part, pltpu.roll(after, LANES - offset, 1))
    return jnp.where(lane < width, part, 0.0)


def join_pieces(piece, count, width, tile, lane):
    low = tile * LANES
    out = None
    for index in range(low // width, min(count, -(-(low + LANES) // width))):
        shift = index * width - low
        part = piece(index)
        if shift % LANES:
            part = pltpu.roll(part, shift % LANES, 1)
        out = part if out is None else jnp.where(lane >= shift, part, out)
    return out


def column_of(ref, layer_index, lanes):
    tall = jnp.broadcast_to(ref[layer_index : layer_index + 1, :], (LANES, LANES)).T
    return jnp.concatenate([tall] * (lanes // LANES), axis=1)


def norm_rows(values, gain_col):
    mean_val = jnp.mean(values, axis=0, keepdims=True)
    centered = values - mean_val
    variance = jnp.mean(centered * centered, axis=0, keepdims=True)
    return (centered * lax.rsqrt(variance + EPSILON) * gain_col).astype(BF16)


def turned(weight):
    return weight.astype(F32).T.astype(BF16)


def select_weights(proj_ref, layer_index, turned_ref, chosen_ref, place, ch):
    for slot in range(4):
        turned_ref[slot] = turned(proj_ref[layer_index, slot])
    for slot in range(4):
        for d in range(NEAR):
            begin = (slot * NEAR + d) * ch
            chosen_ref[begin : begin + ch, :] = turned_ref[slot, place.channels(d, ch), :]


def project_chunk(normed, valid, chosen_ref, near_refs, far_refs, lanes, ch):
    out = jnp.dot(chosen_ref[...], normed, preferred_element_type=F32)
    half = NEAR * ch
    left = (jax.nn.sigmoid(out[half : 2 * half]) * out[:half] * valid).astype(BF16)
    right = (jax.nn.sigmoid(out[3 * half :]) * out[2 * half : 3 * half] * valid).astype(BF16)
    for d in range(NEAR):
        rows = slice(d * ch, (d + 1) * ch)
        near_refs[d][:ch, lanes] = left[rows]
        near_refs[d][ch:, lanes] = right[rows]
        if far_refs:
            far_refs[d][:, lanes] = right[rows]


def chunks_of(total, size):
    return [slice(begin, min(begin + size, total)) for begin in range(0, total, size)]


def first_kernel(
    chunk, own_ref, sibling_ref, valid_ref, gain_ref, proj_ref, *rest
):
    near_refs, far_refs = rest[:NEAR], rest[NEAR : 2 * NEAR]
    turned_pair_ref, normed_ref, pair_ref, turned_ref, chosen_ref = rest[2 * NEAR :]
    place = Place()
    rows, cols = own_ref.shape[:2]
    ch = far_refs[0].shape[0]
    total = valid_ref.shape[1]
    own_at = pl.multiple_of(place.core * cols, 8)
    sibling_at = pl.multiple_of((1 - place.core) * cols, 8)
    pair_ref[:, pl.ds(own_at, cols), :] = own_ref[...].astype(F32)
    pair_ref[:, pl.ds(sibling_at, cols), :] = sibling_ref[...].astype(F32)
    select_weights(proj_ref, 0, turned_ref, chosen_ref, place, ch)
    gain_col = column_of(gain_ref, 0, chunk)
    flat = pair_ref[...].reshape(total, LANES)
    for lanes in chunks_of(total, chunk):
        pair = flat[lanes].T
        turned_pair_ref[:, lanes] = pair.astype(BF16)
        normed = norm_rows(pair, gain_col)
        normed_ref[:, lanes] = normed
        project_chunk(normed, valid_ref[:, lanes], chosen_ref, near_refs, far_refs, lanes, ch)


def finish_chunk(mixed, pair, normed, gain_col, gate, weight):
    normed_out = norm_rows(mixed, gain_col)
    update = jnp.dot(weight, normed_out, preferred_element_type=F32)
    gating = jax.nn.sigmoid(jnp.dot(gate, normed, preferred_element_type=F32))
    return pair.astype(F32) + gating * update


def middle_kernel(chunk, *refs):
    mine, other = refs[:NEAR], refs[NEAR : 2 * NEAR]
    pair_ref, normed_in_ref, valid_ref, gain_ref, out_gain_ref = refs[2 * NEAR : 2 * NEAR + 5]
    proj_ref, gate_ref, weight_ref = refs[2 * NEAR + 5 : 2 * NEAR + 8]
    near_refs = refs[2 * NEAR + 8 : 3 * NEAR + 8]
    after_ref, normed_ref, mixed_ref, turned_ref, chosen_ref = refs[3 * NEAR + 8 :]
    place = Place()
    ch = mine[0].shape[0]
    total = valid_ref.shape[1]
    for d in range(NEAR):
        mixed_ref[place.channels(d, ch), :] = mine[d][...]
        mixed_ref[place.channels(d, ch, True), :] = other[d][...]
    select_weights(proj_ref, 1, turned_ref, chosen_ref, place, ch)
    gate, weight = turned(gate_ref[0]), turned(weight_ref[0])
    out_gain_col = column_of(out_gain_ref, 0, chunk)
    gain_col = column_of(gain_ref, 1, chunk)
    for lanes in chunks_of(total, chunk):
        after = finish_chunk(
            mixed_ref[:, lanes].astype(F32),
            pair_ref[:, lanes],
            normed_in_ref[:, lanes],
            out_gain_col,
            gate,
            weight,
        ).astype(BF16)
        after_ref[:, lanes] = after
        normed = norm_rows(after.astype(F32), gain_col)
        normed_ref[:, lanes] = normed
        project_chunk(normed, valid_ref[:, lanes], chosen_ref, near_refs, (), lanes, ch)


def last_kernel(chunk, *refs):
    mine, other = refs[: 2 * NEAR], refs[2 * NEAR : 4 * NEAR]
    pair_ref, normed_in_ref, out_gain_ref, gate_ref, weight_ref = refs[4 * NEAR : 4 * NEAR + 5]
    out_ref, mixed_ref, after_ref = refs[4 * NEAR + 5 :]
    place = Place()
    ch = mine[0].shape[0]
    total = pair_ref.shape[1]
    rows, cols = out_ref.shape[:2]
    for d in range(NEAR):
        for parts, flag in ((mine, False), (other, True)):
            summed = parts[d][...].astype(F32) + parts[NEAR + d][...].astype(F32)
            mixed_ref[place.channels(d, ch, flag), :] = summed
    gate, weight = turned(gate_ref[1]), turned(weight_ref[1])
    out_gain_col = column_of(out_gain_ref, 1, chunk)
    for lanes in chunks_of(total, chunk):
        after = finish_chunk(
            mixed_ref[:, lanes],
            pair_ref[:, lanes],
            normed_in_ref[:, lanes],
            out_gain_col,
            gate,
            weight,
        )
        after_ref[lanes, :] = after.T
    own_at = pl.multiple_of(place.core * cols, 8)
    for row in range(rows):
        out_ref[row] = after_ref[pl.ds(row * 2 * cols + own_at, cols), :].astype(BF16)


def outgoing_kernel(rows, width, *refs):
    near, far = refs[:NEAR], refs[NEAR : 2 * NEAR]
    outs = refs[2 * NEAR : 3 * NEAR]
    left_ref, right_ref, mixed_ref = refs[3 * NEAR :]
    place = Place()
    ch = far[0].shape[0]
    lane = lane_of(ch)

    def spread(value, ref, side, begin):
        for row in range(rows):
            ref[side, pl.ds(begin + row * ch, ch), :] = take_piece(value, row, width, lane)

    for d in range(NEAR):
        dl, dx = divmod(d, 2)
        for dh, ref in ((0, near[d]), (1, far[d])):
            z = jnp.bitwise_xor(place.z, 2 * dh + dl)
            block = jnp.bitwise_xor(lax.div(z, 2), place.x) * 2 + lax.rem(z, 2)
            begin = pl.multiple_of(block * (rows * ch), 16)
            value = ref[...].astype(F32)
            if dh == 0:
                spread(value[:ch], left_ref, dx, dl * rows * ch)
                value = value[ch:]
            spread(value, right_ref, dx, begin)
    tall = 2 * rows
    for c in range(ch):
        left = jnp.concatenate(
            [left_ref[side, pl.ds(c, tall, stride=ch), :] for side in range(2)], axis=1
        ).astype(BF16)
        for block in range(2):
            begin = block * tall * ch + c
            right = jnp.concatenate(
                [right_ref[side, pl.ds(begin, tall, stride=ch), :] for side in range(2)], axis=1
            ).astype(BF16)
            part = lax.dot_general(
                left, right, (((1,), (1,)), ((), ())), preferred_element_type=F32
            )
            mixed_ref[block, pl.ds(c, tall, stride=ch), :] = jnp.pad(
                part, ((0, 0), (0, LANES - tall))
            )
    for d in range(NEAR):
        dl, dx = divmod(d, 2)
        for tile in range(rows * width // LANES):
            outs[d][:, tile * LANES : (tile + 1) * LANES] = join_pieces(
                lambda row: mixed_ref[dx, pl.ds((dl * rows + row) * ch, ch), :],
                rows,
                width,
                tile,
                lane,
            ).astype(BF16)


def incoming_kernel(rows, width, *refs):
    near = refs[:NEAR]
    outs = refs[NEAR : 3 * NEAR]
    left_ref, right_ref, mixed_ref = refs[3 * NEAR :]
    place = Place()
    ch = outs[0].shape[0]
    lane = lane_of(ch)
    for d in range(NEAR):
        dl, dx = divmod(d, 2)
        value = near[d][...].astype(F32)
        for side, ref in ((value[:ch], left_ref), (value[ch:], right_ref)):
            for row in range(rows):
                ref[dx, pl.ds((dl * rows + row) * ch, ch), :] = take_piece(side, row, width, lane)
    tall = 2 * rows
    for c in range(ch):
        right = jnp.concatenate(
            [right_ref[side, pl.ds(c, tall, stride=ch), :] for side in range(2)], axis=1
        ).astype(BF16)
        for block in range(2):
            left = left_ref[block, pl.ds(c, tall, stride=ch), :].astype(BF16)
            part = lax.dot_general(
                left, right, (((0,), (0,)), ((), ())), preferred_element_type=F32
            )
            for side in range(2):
                mixed_ref[side, pl.ds(block * width * ch + c, width, stride=ch), :] = part[
                    :width, side * LANES : (side + 1) * LANES
                ]
    for d in range(2 * NEAR):
        dz, dx = divmod(d, 2)
        z = jnp.bitwise_xor(place.z, dz)
        block = jnp.bitwise_xor(lax.div(z, 2), place.x) * 2 + lax.rem(z, 2)
        begin = pl.multiple_of(block * (rows * ch), 16)
        for tile in range(rows * width // LANES):
            outs[d][:, tile * LANES : (tile + 1) * LANES] = join_pieces(
                lambda row: mixed_ref[dx, pl.ds(begin + row * ch, ch), :],
                rows,
                width,
                tile,
                lane,
            ).astype(BF16)


def call(kernel, outs, scratch, *args):
    return pl.pallas_call(
        kernel,
        out_shape=[jax.ShapeDtypeStruct(shape, BF16) for shape in outs],
        in_specs=[pl.BlockSpec(memory_space=pltpu.VMEM) for _ in args],
        out_specs=[pl.BlockSpec(memory_space=pltpu.VMEM) for _ in outs],
        scratch_shapes=[pltpu.VMEM(shape, dtype) for shape, dtype in scratch],
        compiler_params=pltpu.CompilerParams(vmem_limit_bytes=24 * 2**20),
    )(*args)


def direct_body(pair_map, token_mask, in_gain, proj_weights, gate_weight, out_gain, out_weight):
    n_row, n_col = lax.axis_size("row"), lax.axis_size("col")
    rows, cols, channels = pair_map.shape
    width = 2 * cols
    total = rows * width
    ch = channels // (2 * NEAR)
    chunk = 5 * LANES

    def swap(value, dz, dx, core=0):
        flip = dz * n_col + dx * 2 + core
        pairs = [(i, i ^ flip) for i in range(n_row * n_col)]
        return lax.ppermute(value, ("row", "col"), pairs)

    def swap_all(values, offset):
        got = [None] * len(values)
        for d in reversed(range(len(values))):
            dz, dx = divmod(d + offset, 2)
            got[d] = swap(values[d], dz, dx) if d + offset else values[d]
        return got

    sibling = swap(pair_map, 0, 0, 1)
    chip_x = lax.div(lax.axis_index("col"), 2)
    valid = pair_mask(
        token_mask, rows, lax.axis_index("row") * rows, width, chip_x * width
    ).reshape(1, total)
    wide = (channels, total)
    weights_scratch = [((4, channels, channels), BF16), ((4 * NEAR * ch, channels), BF16)]

    out = call(
        functools.partial(first_kernel, chunk),
        [(2 * ch, total)] * NEAR + [(ch, total)] * NEAR + [wide, wide],
        [((rows, width, channels), F32)] + weights_scratch,
        pair_map,
        sibling,
        valid,
        in_gain,
        proj_weights,
    )
    far = swap_all(out[NEAR : 2 * NEAR], NEAR)
    near = swap_all(out[:NEAR], 0)
    pair, normed = out[2 * NEAR :]
    tall = 2 * rows
    mixed = call(
        functools.partial(outgoing_kernel, rows, width),
        [(ch, total)] * NEAR,
        [((2, tall * ch, LANES), F32), ((2, 2 * tall * ch, LANES), F32), ((2, tall * ch, LANES), F32)],
        *near,
        *far,
    )
    mixed = swap_all(mixed, 0)
    other = [swap(part, 0, 0, 1) for part in mixed]

    out = call(
        functools.partial(middle_kernel, chunk),
        [(2 * ch, total)] * NEAR + [wide, wide],
        [(wide, BF16)] + weights_scratch,
        *mixed,
        *other,
        pair,
        normed,
        valid,
        in_gain,
        out_gain,
        proj_weights,
        gate_weight,
        out_weight,
    )
    near = swap_all(out[:NEAR], 0)
    pair, normed = out[NEAR:]
    mixed = call(
        functools.partial(incoming_kernel, rows, width),
        [(ch, total)] * (2 * NEAR),
        [((2, tall * ch, LANES), F32), ((2, tall * ch, LANES), F32), ((2, 2 * width * ch, LANES), F32)],
        *near,
    )
    mixed = swap_all(mixed, 0)
    other = [swap(part, 0, 0, 1) for part in mixed]
    return call(
        functools.partial(last_kernel, chunk),
        [(rows, cols, channels)],
        [(wide, F32), ((total, channels), F32)],
        *mixed,
        *other,
        pair,
        normed,
        out_gain,
        gate_weight,
        out_weight,
    )[0]


def solution(mesh):
    in_specs = (P(("groups", "row"), "col", None), P("groups"), P(), P(), P(), P(), P())
    out_specs = P(("groups", "row"), "col", None)
    direct = mesh.shape["row"] == 4 and mesh.shape["col"] == 4
    body = direct_body if direct else gather_body
    return jax.shard_map(body, mesh=mesh, in_specs=in_specs, out_specs=out_specs, check_vma=False)
```

```python
import functools

import jax
import jax.numpy as jnp
from jax import lax
from jax.experimental import pallas as pl
from jax.experimental.pallas import tpu as pltpu
from jax.sharding import PartitionSpec as P

EPSILON = 1e-05
LANES = 128
F32 = jnp.float32
BF16 = jnp.bfloat16


def layer_norm(values, gain_vec):
    mean_val = jnp.mean(values, axis=-1, keepdims=True)
    centered = values - mean_val
    variance = jnp.mean(centered * centered, axis=-1, keepdims=True)
    return centered * jax.lax.rsqrt(variance + EPSILON) * gain_vec


def project_side(pair_tile, pair_valid, layer_index, in_gain, proj_weights, gate_weight):
    normed = layer_norm(pair_tile.astype(F32), in_gain[layer_index]).astype(BF16)
    outputs = [
        jnp.dot(normed, proj_weights[layer_index, slot], preferred_element_type=F32)
        for slot in range(4)
    ]
    weight_mask = pair_valid[..., None]
    left_side = (jax.nn.sigmoid(outputs[1]) * outputs[0] * weight_mask).astype(BF16)
    right_side = (jax.nn.sigmoid(outputs[3]) * outputs[2] * weight_mask).astype(BF16)
    gating = jax.nn.sigmoid(jnp.dot(normed, gate_weight[layer_index], preferred_element_type=F32))
    return (left_side, right_side, gating)


def finish(pair_tile, mixed_sum, gating, layer_index, out_gain, out_weight):
    normed = layer_norm(mixed_sum, out_gain[layer_index]).astype(BF16)
    update = jnp.dot(normed, out_weight[layer_index], preferred_element_type=F32)
    return (pair_tile.astype(F32) + gating * update).astype(BF16)


def pair_mask(token_mask, tile_rows, row_begin, tile_cols, col_begin):
    valid = token_mask.astype(F32)
    row_valid = lax.dynamic_slice_in_dim(valid, row_begin, tile_rows, 0)
    col_valid = lax.dynamic_slice_in_dim(valid, col_begin, tile_cols, 0)
    return row_valid[:, None] * col_valid[None, :]


def gather_body(pair_map, token_mask, in_gain, proj_weights, gate_weight, out_gain, out_weight):
    tile_rows, tile_cols = pair_map.shape[:2]
    pair_valid = pair_mask(
        token_mask,
        tile_rows,
        lax.axis_index("row") * tile_rows,
        tile_cols,
        lax.axis_index("col") * tile_cols,
    )
    left_side, right_side, gating = project_side(
        pair_map, pair_valid, 0, in_gain, proj_weights, gate_weight
    )
    block = lax.all_gather(right_side, "row", axis=0, tiled=True)
    summed = lax.psum_scatter(
        jnp.einsum("jkc,ikc->jic", block, left_side, preferred_element_type=F32).astype(BF16),
        "col",
        scatter_dimension=0,
        tiled=True,
    ).astype(F32)
    mixed = jnp.transpose(summed, (1, 0, 2))
    after_out = finish(pair_map, mixed, gating, 0, out_gain, out_weight)
    left_side, right_side, gating = project_side(
        after_out, pair_valid, 1, in_gain, proj_weights, gate_weight
    )
    block = lax.all_gather(left_side, "col", axis=1, tiled=True)
    mixed = lax.psum_scatter(
        jnp.einsum("kic,kjc->ijc", block, right_side, preferred_element_type=F32).astype(BF16),
        "row",
        scatter_dimension=0,
        tiled=True,
    ).astype(F32)
    return finish(after_out, mixed, gating, 1, out_gain, out_weight)


NEAR = 4


class Place:
    def __init__(self):
        z = lax.axis_index("row")
        col = lax.axis_index("col")
        self.z = z
        self.x = lax.div(col, 2)
        self.core = lax.rem(col, 2)
        self.half = lax.div(z, 2)
        self.group = lax.rem(z, 2) * 2 + self.x

    def channels(self, d, ch, other=False, compact=False, absolute=False):
        core = 1 - self.core if other else self.core
        group = d if absolute else jnp.bitwise_xor(self.group, d)
        begin = group * ch if compact else group * (2 * ch) + core * ch
        return pl.ds(pl.multiple_of(begin, ch), ch)


def lane_of(rows):
    return lax.broadcasted_iota(jnp.int32, (rows, LANES), 1)


def take_piece(value, index, width, lane):
    tile, offset = divmod(index * width, LANES)
    part = value[:, tile * LANES : (tile + 1) * LANES]
    if offset:
        part = pltpu.roll(part, LANES - offset, 1)
    if offset + width > LANES:
        after = value[:, (tile + 1) * LANES : (tile + 2) * LANES]
        part = jnp.where(lane < LANES - offset, part, pltpu.roll(after, LANES - offset, 1))
    return jnp.where(lane < width, part, jnp.zeros_like(part))


def join_pieces(piece, count, width, tile, lane):
    low = tile * LANES
    out = None
    for index in range(low // width, min(count, -(-(low + LANES) // width))):
        shift = index * width - low
        part, begin = piece(index)
        if (shift - begin) % LANES:
            part = pltpu.roll(part, (shift - begin) % LANES, 1)
        out = part if out is None else jnp.where(lane >= shift, part, out)
    return out


def norm_rows(values, gain_col):
    mean_val = jnp.mean(values, axis=0, keepdims=True)
    centered = values - mean_val
    variance = jnp.mean(centered * centered, axis=0, keepdims=True)
    return (centered * lax.rsqrt(variance + EPSILON) * gain_col).astype(BF16)


def turned(weight):
    return weight.astype(F32).T.astype(BF16)


def project_chunk(normed, valid, chosen, lanes):
    out = jnp.dot(chosen, normed, preferred_element_type=F32)
    half = out.shape[0] // 2
    return (jax.nn.sigmoid(out[half:]) * out[:half] * valid).astype(BF16)


def chunks_of(total, size):
    return [slice(begin, min(begin + size, total)) for begin in range(0, total, size)]


def prepare_kernel(
    pair_in,
    mask_in,
    proj_in,
    gate_in,
    weight_in,
    gain_in,
    out_gain_in,
    pair_ref,
    valid_ref,
    chosen_ref,
    gate_ref,
    weight_ref,
    gain_ref,
    out_gain_ref,
    mask_ref,
    proj_ref,
    gates_ref,
    weights_ref,
    gains_ref,
    out_gains_ref,
    turned_ref,
    sems,
):
    moves = [
        (mask_in, mask_ref),
        (proj_in, proj_ref),
        (gain_in, gains_ref),
        (out_gain_in, out_gains_ref),
        (gate_in, gates_ref),
        (weight_in, weights_ref),
        (pair_in, pair_ref),
    ]
    copies = [
        pltpu.make_async_copy(there, here, sems.at[i]) for i, (there, here) in enumerate(moves)
    ]
    for copy in copies:
        copy.start()
    place = Place()
    ch = chosen_ref.shape[1] // (4 * NEAR)
    total = valid_ref.shape[1]
    rows, cols = pair_ref.shape[:2]
    width = 2 * cols
    copies[0].wait()
    lane = lane_of(1)
    mask = mask_ref[...].astype(F32).astype(BF16)

    def lanes_from(begin):
        shape = (mask.shape[1], LANES)
        token = lax.broadcasted_iota(jnp.int32, shape, 0)
        lanes = lax.broadcasted_iota(jnp.int32, shape, 1)
        pick = jnp.where(token == lanes + begin, 1.0, 0.0).astype(BF16)
        return jnp.dot(mask, pick, preferred_element_type=F32)

    col_valid = lanes_from(place.x * width)
    row_valid = lanes_from(place.z * rows)
    for tile in range(total // LANES):
        valid_ref[:, tile * LANES : (tile + 1) * LANES] = join_pieces(
            lambda row: (col_valid * row_valid[:, row : row + 1], 0), rows, width, tile, lane
        )
    copies[1].wait()
    for layer in range(2):
        for slot in range(4):
            turned_ref[slot] = turned(proj_ref[layer, (0, 2, 1, 3)[slot]])
        for slot in range(4):
            for d in range(NEAR):
                begin = (slot * NEAR + d) * ch
                chosen_ref[layer, begin : begin + ch, :] = turned_ref[slot, place.channels(d, ch), :]
    copies[2].wait()
    copies[3].wait()
    for layer in range(2):
        for gains, ref in ((gains_ref, gain_ref), (out_gains_ref, out_gain_ref)):
            ref[layer] = jnp.broadcast_to(gains[layer : layer + 1, :], (LANES, LANES)).T
    copies[4].wait()
    copies[5].wait()
    gate_ref[0] = turned(gates_ref[0])
    weight_ref[0] = turned(weights_ref[0])
    gate_ref[1] = gates_ref[1]
    weight_ref[1] = weights_ref[1]
    copies[6].wait()


def column_of(ref, layer, lanes):
    return jnp.concatenate([ref[layer]] * (-(-lanes // LANES)), axis=1)[:, :lanes]


def chosen_rows(chosen_ref, layer, side):
    half = chosen_ref.shape[1] // 4
    values, gates = (side * half, (side + 1) * half), ((side + 2) * half, (side + 3) * half)
    return jnp.concatenate(
        [chosen_ref[layer, slice(*values), :], chosen_ref[layer, slice(*gates), :]], axis=0
    )


def first_far_kernel(
    chunk, own_ref, sibling_ref, valid_ref, gain_ref, chosen_ref, *rest
):
    far_refs = rest[:NEAR]
    turned_pair_ref, normed_ref, pair_ref = rest[NEAR:]
    place = Place()
    cols = own_ref.shape[1]
    ch = far_refs[0].shape[0]
    total = valid_ref.shape[1]
    own_at = pl.multiple_of(place.core * cols, 8)
    sibling_at = pl.multiple_of((1 - place.core) * cols, 8)
    pair_ref[:, pl.ds(own_at, cols), :] = own_ref[...].astype(F32)
    pair_ref[:, pl.ds(sibling_at, cols), :] = sibling_ref[...].astype(F32)
    gain_col = column_of(gain_ref, 0, chunk)
    flat = pair_ref[...].reshape(total, LANES)
    chosen = chosen_rows(chosen_ref, 0, 1)
    for lanes in chunks_of(total, chunk):
        pair = flat[lanes].T
        turned_pair_ref[:, lanes] = pair.astype(BF16)
        normed = norm_rows(pair, gain_col)
        normed_ref[:, lanes] = normed
        right = project_chunk(normed, valid_ref[:, lanes], chosen, lanes)
        for d in range(NEAR):
            far_refs[d][:, lanes] = right[d * ch : (d + 1) * ch]


def first_near_kernel(chunk, normed_ref, valid_ref, chosen_ref, *rest):
    far_refs, near_refs = rest[:NEAR], rest[NEAR:]
    ch = far_refs[0].shape[0]
    total = valid_ref.shape[1]
    chosen = chosen_rows(chosen_ref, 0, 0)
    for lanes in chunks_of(total, chunk):
        left = project_chunk(normed_ref[:, lanes], valid_ref[:, lanes], chosen, lanes)
        for d in range(NEAR):
            near_refs[d][:ch, lanes] = left[d * ch : (d + 1) * ch]
    for d in range(NEAR):
        near_refs[d][ch:, :] = far_refs[d][...]


def gate_rows(normed_ref, gate, gating_ref, chunk):
    for lanes in chunks_of(normed_ref.shape[1], chunk):
        gating_ref[:, lanes] = jax.nn.sigmoid(
            jnp.dot(gate, normed_ref[:, lanes], preferred_element_type=F32)
        )


def middle_kernel(chunk, *refs):
    mine, other = refs[:NEAR], refs[NEAR : 2 * NEAR]
    pair_ref, gating_ref, valid_ref, gain_ref, out_gain_ref = refs[2 * NEAR : 2 * NEAR + 5]
    chosen_ref, weight_ref = refs[2 * NEAR + 5 : 2 * NEAR + 7]
    near_refs = refs[2 * NEAR + 7 : 3 * NEAR + 7]
    after_ref, normed_ref, mixed_ref = refs[3 * NEAR + 7 :]
    place = Place()
    ch = mine[0].shape[0]
    total = valid_ref.shape[1]
    for d in range(NEAR):
        mixed_ref[place.channels(d, ch), :] = mine[d][...]
        mixed_ref[place.channels(d, ch, True), :] = other[d][...]
    weight = weight_ref[0]
    out_gain_col = column_of(out_gain_ref, 0, chunk)
    gain_col = column_of(gain_ref, 1, chunk)
    sides = [chosen_rows(chosen_ref, 1, side) for side in range(2)]
    for lanes in chunks_of(total, chunk):
        normed_out = norm_rows(mixed_ref[:, lanes].astype(F32), out_gain_col)
        update = jnp.dot(weight, normed_out, preferred_element_type=F32)
        after = (pair_ref[:, lanes].astype(F32) + gating_ref[:, lanes] * update).astype(BF16)
        after_ref[:, lanes] = after
        normed = norm_rows(after.astype(F32), gain_col)
        normed_ref[:, lanes] = normed
        for side in range(2):
            out = project_chunk(normed, valid_ref[:, lanes], sides[side], lanes)
            for d in range(NEAR):
                near_refs[d][side * ch : (side + 1) * ch, lanes] = out[d * ch : (d + 1) * ch]


def own_kernel(chunk, cols, after_ref, normed_ref, gate_ref, own_ref, gating_ref, rows_ref):
    place = Place()
    total = after_ref.shape[1]
    rows = total // (2 * cols)
    own_at = pl.multiple_of(place.core * cols, 8)
    for lanes in chunks_of(total, chunk):
        rows_ref[0, lanes, :] = after_ref[:, lanes].astype(F32).T
        rows_ref[1, lanes, :] = lax.dot_general(
            normed_ref[:, lanes],
            gate_ref[1],
            (((0,), (0,)), ((), ())),
            preferred_element_type=F32,
        )
    for row in range(rows):
        here = pl.ds(row * 2 * cols + own_at, cols)
        own_ref[row * cols : (row + 1) * cols, :] = rows_ref[0, here, :]
        gating_ref[row * cols : (row + 1) * cols, :] = jax.nn.sigmoid(rows_ref[1, here, :])


def sum_kernel(*refs):
    near, far = refs[:NEAR], refs[NEAR : 2 * NEAR]
    keep_ref, send_ref = refs[2 * NEAR :]
    place = Place()
    ch = near[0].shape[0]
    half = keep_ref.shape[1]
    begin = half // LANES * LANES
    for d in range(NEAR):
        total = near[d][...].astype(F32) + far[d][:, : 2 * half].astype(F32)
        rows = place.channels(d, ch, compact=True)
        first = total[:, :half]
        second = pltpu.roll(total[:, begin:], half, 1)[:, :half]
        keep_ref[rows, :] = jnp.where(place.core == 0, first, second).astype(BF16)
        send_ref[rows, :] = jnp.where(place.core == 0, second, first).astype(BF16)


def last_kernel(chunk, keep_ref, got_ref, own_ref, gating_ref, gain_ref, weight_ref, out_ref, mixed_ref):
    place = Place()
    ch = keep_ref.shape[0] // NEAR
    for group in range(NEAR):
        rows = slice(group * ch, (group + 1) * ch)
        mixed_ref[place.channels(group, ch, absolute=True), :] = keep_ref[rows, :]
        mixed_ref[place.channels(group, ch, True, absolute=True), :] = got_ref[rows, :]
    for lanes in chunks_of(keep_ref.shape[1], chunk):
        gain_col = column_of(gain_ref, 1, lanes.stop - lanes.start)
        normed = norm_rows(mixed_ref[:, lanes].astype(F32), gain_col)
        update = lax.dot_general(
            normed, weight_ref[1], (((0,), (0,)), ((), ())), preferred_element_type=F32
        )
        out_ref[lanes, :] = (own_ref[lanes, :] + gating_ref[lanes, :] * update).astype(BF16)


def unpack(value, ref, begin, rows, width, lane):
    ch = value.shape[0]
    for row in range(rows):
        ref[pl.ds(begin + row * ch, ch), :] = take_piece(value, row, width, lane).astype(F32)


def pack(ref, begin, out_ref, rows, width, lane):
    ch = out_ref.shape[0]
    for tile in range(rows * width // LANES):
        out_ref[:, tile * LANES : (tile + 1) * LANES] = join_pieces(
            lambda row: (ref[pl.ds(begin + row * ch, ch), :].astype(BF16), 0), rows, width, tile, lane
        )


def pack_halves(ref, begin, out_ref, rows, cols, lane):
    ch = out_ref.shape[0]
    for tile in range(out_ref.shape[1] // LANES):
        lanes = slice(tile * LANES, (tile + 1) * LANES)
        if tile * LANES >= 2 * rows * cols:
            out_ref[:, lanes] = jnp.zeros((ch, LANES), BF16)
            continue

        def piece(index):
            part = ref[pl.ds(begin + (index % rows) * ch, ch), :].astype(BF16)
            return part, index // rows * cols

        out_ref[:, lanes] = join_pieces(piece, 2 * rows, cols, tile, lane)


def channel_of(ref, c, ch, tall):
    return jnp.concatenate(
        [ref[side, pl.ds(c, tall, stride=ch), :] for side in range(2)], axis=1
    ).astype(BF16)


def widen(part):
    return jnp.pad(part, ((0, 0), (0, LANES - part.shape[1])))


def outgoing_multiply(left_ref, right_ref, mixed_ref, ch, tall):
    for c in range(ch):
        left = channel_of(left_ref, c, ch, tall)
        right = channel_of(right_ref, c, ch, tall)
        part = lax.dot_general(left, right, (((1,), (1,)), ((), ())), preferred_element_type=F32)
        mixed_ref[pl.ds(c, tall, stride=ch), :] = widen(part)


def outgoing_near_kernel(rows, width, *refs):
    near, (normed_ref, gate_ref) = refs[:NEAR], refs[NEAR : NEAR + 2]
    gating_ref, left_ref, *outs = refs[NEAR + 2 : NEAR + 6]
    right_ref, mixed_ref = refs[NEAR + 6 :]
    gate_rows(normed_ref, gate_ref[0], gating_ref, 5 * LANES)
    place = Place()
    ch = outs[0].shape[0]
    lane = lane_of(ch)
    for d in range(NEAR):
        dl, dx = divmod(d, 2)
        value = near[d][...]
        unpack(value[:ch], left_ref.at[dx], dl * rows * ch, rows, width, lane)
        low = jnp.bitwise_xor(lax.rem(place.z, 2), dl)
        begin = pl.multiple_of(low * (rows * ch), 16)
        unpack(value[ch:], right_ref.at[dx], begin, rows, width, lane)
    outgoing_multiply(left_ref, right_ref, mixed_ref, ch, 2 * rows)
    for dl in range(2):
        pack(mixed_ref, dl * rows * ch, outs[dl], rows, width, lane)


def outgoing_far_kernel(rows, width, *refs):
    far, left_ref, done = refs[:NEAR], refs[NEAR], refs[NEAR + 1 : NEAR + 3]
    outs = refs[NEAR + 3 : 2 * NEAR + 3]
    right_ref, mixed_ref = refs[2 * NEAR + 3 :]
    place = Place()
    ch = far[0].shape[0]
    lane = lane_of(ch)
    for d in range(NEAR):
        dl, dx = divmod(d, 2)
        low = jnp.bitwise_xor(lax.rem(place.z, 2), dl)
        begin = pl.multiple_of(low * (rows * ch), 16)
        unpack(far[d][...], right_ref.at[dx], begin, rows, width, lane)
    outgoing_multiply(left_ref, right_ref, mixed_ref, ch, 2 * rows)
    same = jnp.bitwise_xor(place.half, place.x)
    for dx in range(2):

        @pl.when(same == dx)
        def _(dx=dx):
            for dl in range(2):
                outs[2 * dl + dx][...] = done[dl][...]
                pack(mixed_ref, dl * rows * ch, outs[2 * dl + 1 - dx], rows, width, lane)


def incoming_kernel(rows, width, dh, *refs):
    near = refs[:NEAR]
    outs = refs[NEAR : 2 * NEAR]
    left_ref, right_ref, mixed_ref = refs[2 * NEAR :]
    place = Place()
    ch = outs[0].shape[0]
    lane = lane_of(ch)
    wanted = jnp.bitwise_xor(jnp.bitwise_xor(place.half, dh), place.x)
    for d in range(NEAR):
        dl, dx = divmod(d, 2)
        begin = dl * rows * ch
        unpack(near[d][ch:, :], right_ref.at[dx], begin, rows, width, lane)

        @pl.when(wanted == dx)
        def _(d=d, begin=begin):
            unpack(near[d][:ch, :], left_ref, begin, rows, width, lane)

    tall = 2 * rows
    for c in range(ch):
        right = channel_of(right_ref, c, ch, tall)
        left = left_ref[pl.ds(c, tall, stride=ch), :].astype(BF16)
        part = lax.dot_general(left, right, (((0,), (0,)), ((), ())), preferred_element_type=F32)
        for side in range(2):
            mixed_ref[side, pl.ds(c, width, stride=ch), :] = part[
                :width, side * LANES : (side + 1) * LANES
            ]
    for d in range(NEAR):
        dl, dx = divmod(d, 2)
        low = jnp.bitwise_xor(lax.rem(place.z, 2), dl)
        begin = pl.multiple_of(low * (rows * ch), 16)
        pack_halves(mixed_ref.at[dx], begin, outs[d], rows, width // 2, lane)


def call(kernel, micros, outs, scratch, *args, space=pltpu.VMEM):
    outs = [(out, BF16) if isinstance(out[0], int) else out for out in outs]
    if space is pltpu.HBM:
        args = [pltpu.with_memory_space_constraint(arg, space) for arg in args]
    return pl.pallas_call(
        kernel,
        out_shape=[jax.ShapeDtypeStruct(shape, dtype) for shape, dtype in outs],
        in_specs=[pl.BlockSpec(memory_space=space) for _ in args],
        out_specs=[pl.BlockSpec(memory_space=pltpu.VMEM) for _ in outs],
        scratch_shapes=[
            entry if not isinstance(entry, tuple) else pltpu.VMEM(*entry) for entry in scratch
        ],
        compiler_params=pltpu.CompilerParams(vmem_limit_bytes=24 * 2**20),
        cost_estimate=pl.CostEstimate(
            flops=int(micros * 1.1e9), bytes_accessed=0, transcendentals=0
        ),
    )(*args)


def direct_body(pair_map, token_mask, in_gain, proj_weights, gate_weight, out_gain, out_weight):
    n_row, n_col = lax.axis_size("row"), lax.axis_size("col")
    rows, cols, channels = pair_map.shape
    width = 2 * cols
    total = rows * width
    ch = channels // (2 * NEAR)
    chunk = 5 * LANES

    def swap(value, dz, dx, core=0):
        flip = dz * n_col + dx * 2 + core
        pairs = [(i, i ^ flip) for i in range(n_row * n_col)]
        return lax.ppermute(value, ("row", "col"), pairs)

    def swap_all(values, offset):
        return [
            swap(value, *divmod(d + offset, 2)) if d + offset else value
            for d, value in enumerate(values)
        ]

    sibling = swap(pair_map, 0, 0, 1)
    wide = (channels, total)
    square = (channels, channels)
    mask = token_mask.reshape(1, -1)
    own, valid, chosen, gates, weights, gains, out_gains = call(
        prepare_kernel,
        1.5,
        [
            pair_map.shape,
            ((1, total), F32),
            (2, 4 * NEAR * ch, channels),
            (2, *square),
            (2, *square),
            ((2, *square), F32),
            ((2, *square), F32),
        ],
        [
            (mask.shape, mask.dtype),
            (proj_weights.shape, BF16),
            (gate_weight.shape, BF16),
            (out_weight.shape, BF16),
            (in_gain.shape, F32),
            (out_gain.shape, F32),
            ((4, *square), BF16),
            pltpu.SemaphoreType.DMA((7,)),
        ],
        pair_map,
        mask,
        proj_weights,
        gate_weight,
        out_weight,
        in_gain,
        out_gain,
        space=pltpu.HBM,
    )
    *right, pair, normed = call(
        functools.partial(first_far_kernel, chunk),
        1.0,
        [(ch, total)] * NEAR + [wide, wide],
        [((rows, width, channels), F32)],
        own,
        sibling,
        valid,
        gains,
        chosen,
    )
    near = call(
        functools.partial(first_near_kernel, chunk),
        0.6,
        [(2 * ch, total)] * NEAR,
        [],
        normed,
        valid,
        chosen,
        *right,
    )
    far = swap_all(right, NEAR)
    near = swap_all(near, 0)
    tall = 2 * rows
    side = ((tall * ch, LANES), F32)
    sides = ((2, tall * ch, LANES), F32)
    gating, left, *mixed = call(
        functools.partial(outgoing_near_kernel, rows, width),
        2.0,
        [(wide, F32), sides] + [(ch, total)] * 2,
        [sides, side],
        *near,
        normed,
        gates,
    )
    mixed = call(
        functools.partial(outgoing_far_kernel, rows, width),
        1.2,
        [(ch, total)] * NEAR,
        [sides, side],
        *far,
        left,
        *mixed,
    )
    mixed = swap_all(mixed, 0)
    other = [swap(part, 0, 0, 1) for part in mixed]

    *near, pair, normed = call(
        functools.partial(middle_kernel, chunk),
        2.3,
        [(2 * ch, total)] * NEAR + [wide, wide],
        [(wide, BF16)],
        *mixed,
        *other,
        pair,
        gating,
        valid,
        gains,
        out_gains,
        chosen,
        weights,
    )
    near = swap_all(near, 0)
    half = rows * cols
    parts = [
        call(
            functools.partial(incoming_kernel, rows, width, dh),
            2.0,
            [(ch, total)] * NEAR,
            [side, sides, ((2, width * ch, LANES), F32)],
            *near,
        )
        for dh in range(2)
    ]
    own, gating = call(
        functools.partial(own_kernel, chunk, cols),
        2.0,
        [((half, channels), F32)] * 2,
        [((2, total, channels), F32)],
        pair,
        normed,
        gates,
    )
    mixed = swap_all(parts[0], 0) + swap_all(parts[1], NEAR)
    keep, send = call(sum_kernel, 1.0, [(NEAR * ch, half)] * 2, [], *mixed)
    got = swap(send, 0, 0, 1)
    out = call(
        functools.partial(last_kernel, chunk),
        1.0,
        [(half, channels)],
        [((channels, half), BF16)],
        keep,
        got,
        own,
        gating,
        out_gains,
        weights,
    )[0]
    return out.reshape(rows, cols, channels)


def solution(mesh):
    in_specs = (P(("groups", "row"), "col", None), P("groups"), P(), P(), P(), P(), P())
    out_specs = P(("groups", "row"), "col", None)
    direct = mesh.shape["row"] == 4 and mesh.shape["col"] == 4
    body = direct_body if direct else gather_body
    return jax.shard_map(body, mesh=mesh, in_specs=in_specs, out_specs=out_specs, check_vma=False)
```

```python
import functools

import jax
import jax.numpy as jnp
from jax import lax
from jax.experimental import pallas as pl
from jax.experimental.pallas import tpu as pltpu
from jax.sharding import PartitionSpec as P

EPSILON = 1e-05
LANES = 128
F32 = jnp.float32
BF16 = jnp.bfloat16


def layer_norm(values, gain_vec):
    mean_val = jnp.mean(values, axis=-1, keepdims=True)
    centered = values - mean_val
    variance = jnp.mean(centered * centered, axis=-1, keepdims=True)
    return centered * jax.lax.rsqrt(variance + EPSILON) * gain_vec


def project_side(pair_tile, pair_valid, layer_index, in_gain, proj_weights, gate_weight):
    normed = layer_norm(pair_tile.astype(F32), in_gain[layer_index]).astype(BF16)
    outputs = [
        jnp.dot(normed, proj_weights[layer_index, slot], preferred_element_type=F32)
        for slot in range(4)
    ]
    weight_mask = pair_valid[..., None]
    left_side = (jax.nn.sigmoid(outputs[1]) * outputs[0] * weight_mask).astype(BF16)
    right_side = (jax.nn.sigmoid(outputs[3]) * outputs[2] * weight_mask).astype(BF16)
    gating = jax.nn.sigmoid(jnp.dot(normed, gate_weight[layer_index], preferred_element_type=F32))
    return (left_side, right_side, gating)


def finish(pair_tile, mixed_sum, gating, layer_index, out_gain, out_weight):
    normed = layer_norm(mixed_sum, out_gain[layer_index]).astype(BF16)
    update = jnp.dot(normed, out_weight[layer_index], preferred_element_type=F32)
    return (pair_tile.astype(F32) + gating * update).astype(BF16)


def pair_mask(token_mask, tile_rows, row_begin, tile_cols, col_begin):
    valid = token_mask.astype(F32)
    row_valid = lax.dynamic_slice_in_dim(valid, row_begin, tile_rows, 0)
    col_valid = lax.dynamic_slice_in_dim(valid, col_begin, tile_cols, 0)
    return row_valid[:, None] * col_valid[None, :]


def gather_body(pair_map, token_mask, in_gain, proj_weights, gate_weight, out_gain, out_weight):
    tile_rows, tile_cols = pair_map.shape[:2]
    pair_valid = pair_mask(
        token_mask,
        tile_rows,
        lax.axis_index("row") * tile_rows,
        tile_cols,
        lax.axis_index("col") * tile_cols,
    )
    left_side, right_side, gating = project_side(
        pair_map, pair_valid, 0, in_gain, proj_weights, gate_weight
    )
    block = lax.all_gather(right_side, "row", axis=0, tiled=True)
    summed = lax.psum_scatter(
        jnp.einsum("jkc,ikc->jic", block, left_side, preferred_element_type=F32).astype(BF16),
        "col",
        scatter_dimension=0,
        tiled=True,
    ).astype(F32)
    mixed = jnp.transpose(summed, (1, 0, 2))
    after_out = finish(pair_map, mixed, gating, 0, out_gain, out_weight)
    left_side, right_side, gating = project_side(
        after_out, pair_valid, 1, in_gain, proj_weights, gate_weight
    )
    block = lax.all_gather(left_side, "col", axis=1, tiled=True)
    mixed = lax.psum_scatter(
        jnp.einsum("kic,kjc->ijc", block, right_side, preferred_element_type=F32).astype(BF16),
        "row",
        scatter_dimension=0,
        tiled=True,
    ).astype(F32)
    return finish(after_out, mixed, gating, 1, out_gain, out_weight)


NEAR = 4
RIGHT_NEAR = (0, 1, 2, 3)
RIGHT_FAR = (0, 1, 2, 3)
OUTGOING = (0, 3, 2, 1)
INCOMING = (0, 2, 1, 3)
SUMS_NEAR = (0, 3, 2, 1)
SUMS_FAR = (1, 0, 3, 2)


def ordered(values, order):
    return [values[d] for d in order]


def restored(values, order):
    return [values[order.index(d)] for d in range(NEAR)]


class Place:
    def __init__(self):
        z = lax.axis_index("row")
        col = lax.axis_index("col")
        self.z = z
        self.x = lax.div(col, 2)
        self.core = lax.rem(col, 2)
        self.half = lax.div(z, 2)
        self.group = lax.rem(z, 2) * 2 + self.x

    def channels(self, d, ch, other=False, compact=False, absolute=False):
        core = 1 - self.core if other else self.core
        group = d if absolute else jnp.bitwise_xor(self.group, d)
        begin = group * ch if compact else group * (2 * ch) + core * ch
        return pl.ds(pl.multiple_of(begin, ch), ch)


def lane_of(rows):
    return lax.broadcasted_iota(jnp.int32, (rows, LANES), 1)


def take_piece(value, index, width, lane):
    tile, offset = divmod(index * width, LANES)
    part = value[:, tile * LANES : (tile + 1) * LANES]
    if offset:
        part = pltpu.roll(part, LANES - offset, 1)
    if offset + width > LANES:
        after = value[:, (tile + 1) * LANES : (tile + 2) * LANES]
        part = jnp.where(lane < LANES - offset, part, pltpu.roll(after, LANES - offset, 1))
    return jnp.where(lane < width, part, jnp.zeros_like(part))


def join_pieces(piece, count, width, tile, lane):
    low = tile * LANES
    out = None
    for index in range(low // width, min(count, -(-(low + LANES) // width))):
        shift = index * width - low
        part, begin = piece(index)
        if (shift - begin) % LANES:
            part = pltpu.roll(part, (shift - begin) % LANES, 1)
        out = part if out is None else jnp.where(lane >= shift, part, out)
    return out


def norm_rows(values, gain_col, valid=None):
    mean_val = jnp.mean(values, axis=0, keepdims=True)
    centered = values - mean_val
    variance = jnp.mean(centered * centered, axis=0, keepdims=True)
    scale = lax.rsqrt(variance + EPSILON)
    if valid is not None:
        scale = scale * valid
    return (centered * scale * gain_col).astype(BF16)


def turned(weight):
    return weight.astype(F32).T.astype(BF16)


def halved(weight):
    return (weight.astype(F32) * 0.5).astype(BF16)


def project_chunk(normed, chosen):
    out = jnp.dot(chosen, normed, preferred_element_type=F32)
    half = out.shape[0] // 2
    return ((jnp.tanh(out[half:]) + 1.0) * out[:half]).astype(BF16)


def chunks_of(total, size):
    return [slice(begin, min(begin + size, total)) for begin in range(0, total, size)]


def prepare_kernel(
    pair_in,
    mask_in,
    proj_in,
    gate_in,
    weight_in,
    gain_in,
    out_gain_in,
    pair_ref,
    valid_ref,
    chosen_ref,
    gate_ref,
    weight_ref,
    gain_ref,
    out_gain_ref,
    mask_ref,
    proj_ref,
    gates_ref,
    weights_ref,
    gains_ref,
    out_gains_ref,
    turned_ref,
    sems,
):
    moves = [
        (mask_in, mask_ref),
        (proj_in, proj_ref),
        (gain_in, gains_ref),
        (out_gain_in, out_gains_ref),
        (gate_in, gates_ref),
        (weight_in, weights_ref),
        (pair_in, pair_ref),
    ]
    copies = [
        pltpu.make_async_copy(there, here, sems.at[i]) for i, (there, here) in enumerate(moves)
    ]
    for copy in copies:
        copy.start()
    place = Place()
    ch = chosen_ref.shape[1] // (4 * NEAR)
    total = valid_ref.shape[1]
    rows, cols = pair_ref.shape[:2]
    width = 2 * cols
    copies[0].wait()
    lane = lane_of(1)
    mask = mask_ref[...].astype(F32).astype(BF16)

    def lanes_from(begin):
        shape = (mask.shape[1], LANES)
        token = lax.broadcasted_iota(jnp.int32, shape, 0)
        lanes = lax.broadcasted_iota(jnp.int32, shape, 1)
        pick = jnp.where(token == lanes + begin, 1.0, 0.0).astype(BF16)
        return jnp.dot(mask, pick, preferred_element_type=F32)

    col_valid = lanes_from(place.x * width)
    row_valid = lanes_from(place.z * rows)
    for tile in range(total // LANES):
        valid_ref[:, tile * LANES : (tile + 1) * LANES] = join_pieces(
            lambda row: (col_valid * row_valid[:, row : row + 1], 0), rows, width, tile, lane
        )
    copies[1].wait()
    for layer in range(2):
        for slot in range(4):
            turned_ref[slot] = halved(turned(proj_ref[layer, (0, 2, 1, 3)[slot]]))
        for slot in range(4):
            for d in range(NEAR):
                begin = (slot * NEAR + d) * ch
                chosen_ref[layer, begin : begin + ch, :] = turned_ref[slot, place.channels(d, ch), :]
    copies[2].wait()
    copies[3].wait()
    for layer in range(2):
        for gains, ref in ((gains_ref, gain_ref), (out_gains_ref, out_gain_ref)):
            ref[layer] = jnp.broadcast_to(gains[layer : layer + 1, :], (LANES, LANES)).T
    copies[4].wait()
    copies[5].wait()
    gate_ref[0] = halved(turned(gates_ref[0]))
    weight_ref[0] = halved(turned(weights_ref[0]))
    gate_ref[1] = halved(gates_ref[1])
    weight_ref[1] = halved(weights_ref[1])
    copies[6].wait()


def column_of(ref, layer, lanes):
    return jnp.concatenate([ref[layer]] * (-(-lanes // LANES)), axis=1)[:, :lanes]


def chosen_rows(chosen_ref, layer, side):
    half = chosen_ref.shape[1] // 4
    values, gates = (side * half, (side + 1) * half), ((side + 2) * half, (side + 3) * half)
    return jnp.concatenate(
        [chosen_ref[layer, slice(*values), :], chosen_ref[layer, slice(*gates), :]], axis=0
    )


def first_far_kernel(
    chunk, own_ref, sibling_ref, valid_ref, gain_ref, chosen_ref, *rest
):
    far_refs = rest[:NEAR]
    turned_pair_ref, normed_ref, pair_ref = rest[NEAR:]
    place = Place()
    cols = own_ref.shape[1]
    ch = far_refs[0].shape[0]
    total = valid_ref.shape[1]
    own_at = pl.multiple_of(place.core * cols, 8)
    sibling_at = pl.multiple_of((1 - place.core) * cols, 8)
    pair_ref[:, pl.ds(own_at, cols), :] = own_ref[...].astype(F32)
    pair_ref[:, pl.ds(sibling_at, cols), :] = sibling_ref[...].astype(F32)
    gain_col = column_of(gain_ref, 0, chunk)
    flat = pair_ref[...].reshape(total, LANES)
    chosen = chosen_rows(chosen_ref, 0, 1)
    for lanes in chunks_of(total, chunk):
        pair = flat[lanes].T
        turned_pair_ref[:, lanes] = pair.astype(BF16)
        normed = norm_rows(pair, gain_col[:, : lanes.stop - lanes.start], valid_ref[:, lanes])
        normed_ref[:, lanes] = normed
        right = project_chunk(normed, chosen)
        for d in range(NEAR):
            far_refs[d][:, lanes] = right[d * ch : (d + 1) * ch]


def first_near_kernel(chunk, normed_ref, chosen_ref, *rest):
    far_refs, near_refs = rest[:NEAR], rest[NEAR:]
    ch = far_refs[0].shape[0]
    total = normed_ref.shape[1]
    chosen = chosen_rows(chosen_ref, 0, 0)
    for lanes in chunks_of(total, chunk):
        left = project_chunk(normed_ref[:, lanes], chosen)
        for d in range(NEAR):
            near_refs[d][:ch, lanes] = left[d * ch : (d + 1) * ch]
    for d in range(NEAR):
        near_refs[d][ch:, :] = far_refs[d][...]


def gate_rows(normed_ref, gate, gating_ref, chunk):
    for lanes in chunks_of(normed_ref.shape[1], chunk):
        gating_ref[:, lanes] = 1.0 + jnp.tanh(
            jnp.dot(gate, normed_ref[:, lanes], preferred_element_type=F32)
        )


def middle_kernel(chunk, *refs):
    mine = restored(refs[:NEAR], OUTGOING)
    other = restored(refs[NEAR : 2 * NEAR], OUTGOING)
    pair_ref, gating_ref, valid_ref, gain_ref, out_gain_ref = refs[2 * NEAR : 2 * NEAR + 5]
    chosen_ref, weight_ref = refs[2 * NEAR + 5 : 2 * NEAR + 7]
    near_refs = refs[2 * NEAR + 7 : 3 * NEAR + 7]
    after_ref, normed_ref, mixed_ref = refs[3 * NEAR + 7 :]
    place = Place()
    ch = mine[0].shape[0]
    total = valid_ref.shape[1]
    for d in range(NEAR):
        mixed_ref[place.channels(d, ch), :] = mine[d][...]
        mixed_ref[place.channels(d, ch, True), :] = other[d][...]
    weight = weight_ref[0]
    out_gain_col = column_of(out_gain_ref, 0, chunk)
    gain_col = column_of(gain_ref, 1, chunk)
    sides = [chosen_rows(chosen_ref, 1, side) for side in range(2)]
    for lanes in chunks_of(total, chunk):
        normed_out = norm_rows(
            mixed_ref[:, lanes].astype(F32), out_gain_col[:, : lanes.stop - lanes.start]
        )
        update = jnp.dot(weight, normed_out, preferred_element_type=F32)
        after = (pair_ref[:, lanes].astype(F32) + gating_ref[:, lanes] * update).astype(BF16)
        after_ref[:, lanes] = after
        normed = norm_rows(
            after.astype(F32), gain_col[:, : lanes.stop - lanes.start], valid_ref[:, lanes]
        )
        normed_ref[:, lanes] = normed
        for side in range(2):
            out = project_chunk(normed, sides[side])
            for d in range(NEAR):
                near_refs[d][side * ch : (side + 1) * ch, lanes] = out[d * ch : (d + 1) * ch]


def own_kernel(chunk, cols, after_ref, normed_ref, gate_ref, own_ref, gating_ref, rows_ref):
    place = Place()
    total = after_ref.shape[1]
    rows = total // (2 * cols)
    own_at = pl.multiple_of(place.core * cols, 8)
    for lanes in chunks_of(total, chunk):
        rows_ref[0, lanes, :] = after_ref[:, lanes].astype(F32).T
        rows_ref[1, lanes, :] = lax.dot_general(
            normed_ref[:, lanes],
            gate_ref[1],
            (((0,), (0,)), ((), ())),
            preferred_element_type=F32,
        )
    for row in range(rows):
        here = pl.ds(row * 2 * cols + own_at, cols)
        own_ref[row * cols : (row + 1) * cols, :] = rows_ref[0, here, :]
        gating_ref[row * cols : (row + 1) * cols, :] = 1.0 + jnp.tanh(rows_ref[1, here, :])


def sum_kernel(*refs):
    near = restored(refs[:NEAR], SUMS_NEAR)
    far = restored(refs[NEAR : 2 * NEAR], SUMS_FAR)
    keep_ref, send_ref = refs[2 * NEAR :]
    place = Place()
    ch = near[0].shape[0]
    half = keep_ref.shape[1]
    begin = half // LANES * LANES
    for d in range(NEAR):
        total = near[d][...].astype(F32) + far[d][:, : 2 * half].astype(F32)
        rows = place.channels(d, ch, compact=True)
        first = total[:, :half]
        second = pltpu.roll(total[:, begin:], half, 1)[:, :half]
        keep_ref[rows, :] = jnp.where(place.core == 0, first, second).astype(BF16)
        send_ref[rows, :] = jnp.where(place.core == 0, second, first).astype(BF16)


def last_kernel(chunk, keep_ref, got_ref, own_ref, gating_ref, gain_ref, weight_ref, out_ref, mixed_ref):
    place = Place()
    ch = keep_ref.shape[0] // NEAR
    for group in range(NEAR):
        rows = slice(group * ch, (group + 1) * ch)
        mixed_ref[place.channels(group, ch, absolute=True), :] = keep_ref[rows, :]
        mixed_ref[place.channels(group, ch, True, absolute=True), :] = got_ref[rows, :]
    for lanes in chunks_of(keep_ref.shape[1], chunk):
        gain_col = column_of(gain_ref, 1, lanes.stop - lanes.start)
        normed = norm_rows(mixed_ref[:, lanes].astype(F32), gain_col)
        update = lax.dot_general(
            normed, weight_ref[1], (((0,), (0,)), ((), ())), preferred_element_type=F32
        )
        out_ref[lanes, :] = (own_ref[lanes, :] + gating_ref[lanes, :] * update).astype(BF16)


def unpack(value, ref, begin, rows, width, lane):
    ch = value.shape[0]
    for row in range(rows):
        ref[pl.ds(begin + row * ch, ch), :] = take_piece(value, row, width, lane).astype(F32)


def pack(ref, begin, out_ref, rows, width, lane):
    ch = out_ref.shape[0]
    for tile in range(rows * width // LANES):
        out_ref[:, tile * LANES : (tile + 1) * LANES] = join_pieces(
            lambda row: (ref[pl.ds(begin + row * ch, ch), :].astype(BF16), 0), rows, width, tile, lane
        )


def pack_halves(ref, begin, out_ref, rows, cols, lane):
    ch = out_ref.shape[0]
    for tile in range(out_ref.shape[1] // LANES):
        lanes = slice(tile * LANES, (tile + 1) * LANES)
        if tile * LANES >= 2 * rows * cols:
            out_ref[:, lanes] = jnp.zeros((ch, LANES), BF16)
            continue

        def piece(index):
            part = ref[pl.ds(begin + (index % rows) * ch, ch), :].astype(BF16)
            return part, index // rows * cols

        out_ref[:, lanes] = join_pieces(piece, 2 * rows, cols, tile, lane)


def channel_of(ref, c, ch, tall):
    return jnp.concatenate(
        [ref[side, pl.ds(c, tall, stride=ch), :] for side in range(ref.shape[0])], axis=1
    ).astype(BF16)


def widen(part):
    return jnp.pad(part, ((0, 0), (0, LANES - part.shape[1])))


def outgoing_multiply(left_ref, right_ref, mixed_ref, ch, tall):
    for c in range(ch):
        left = channel_of(left_ref, c, ch, tall)
        right = channel_of(right_ref, c, ch, tall)
        part = lax.dot_general(left, right, (((1,), (1,)), ((), ())), preferred_element_type=F32)
        mixed_ref[pl.ds(c, tall, stride=ch), :] = widen(part)


def outgoing_near_kernel(rows, width, *refs):
    near = restored(refs[:NEAR], RIGHT_NEAR)
    normed_ref, gate_ref = refs[NEAR : NEAR + 2]
    gating_ref, left_ref, *outs = refs[NEAR + 2 : NEAR + 6]
    right_ref, mixed_ref = refs[NEAR + 6 :]
    gate_rows(normed_ref, gate_ref[0], gating_ref, 13 * LANES)
    place = Place()
    ch = outs[0].shape[0]
    lane = lane_of(ch)
    for d in range(NEAR):
        dl, dx = divmod(d, 2)
        value = near[d][...]
        unpack(value[:ch], left_ref.at[dx], dl * rows * ch, rows, width, lane)
        low = jnp.bitwise_xor(lax.rem(place.z, 2), dl)
        begin = pl.multiple_of(low * (rows * ch), 16)
        unpack(value[ch:], right_ref.at[dx], begin, rows, width, lane)
    outgoing_multiply(left_ref, right_ref, mixed_ref, ch, 2 * rows)
    for dl in range(2):
        pack(mixed_ref, dl * rows * ch, outs[dl], rows, width, lane)


def outgoing_far_kernel(rows, width, *refs):
    far = restored(refs[:NEAR], RIGHT_FAR)
    left_ref, done = refs[NEAR], refs[NEAR + 1 : NEAR + 3]
    outs = refs[NEAR + 3 : 2 * NEAR + 3]
    right_ref, mixed_ref = refs[2 * NEAR + 3 :]
    place = Place()
    ch = far[0].shape[0]
    lane = lane_of(ch)
    for d in range(NEAR):
        dl, dx = divmod(d, 2)
        low = jnp.bitwise_xor(lax.rem(place.z, 2), dl)
        begin = pl.multiple_of(low * (rows * ch), 16)
        unpack(far[d][...], right_ref.at[dx], begin, rows, width, lane)
    outgoing_multiply(left_ref, right_ref, mixed_ref, ch, 2 * rows)
    same = jnp.bitwise_xor(place.half, place.x)
    for dx in range(2):

        @pl.when(same == dx)
        def _(dx=dx):
            for dl in range(2):
                outs[2 * dl + dx][...] = done[dl][...]
                pack(mixed_ref, dl * rows * ch, outs[2 * dl + 1 - dx], rows, width, lane)


def incoming_kernel(rows, width, dh, sides, *refs):
    near, outs, scratch = restored(refs[:NEAR], INCOMING), refs[NEAR:-3], refs[-3:]
    left_ref, right_ref, mixed_ref = scratch
    place = Place()
    ch = outs[0].shape[0]
    lane = lane_of(ch)
    wanted = jnp.bitwise_xor(jnp.bitwise_xor(place.half, dh), place.x)
    for d in range(NEAR):
        dl, dx = divmod(d, 2)
        begin = dl * rows * ch
        if dx in sides:
            at = right_ref.at[sides.index(dx)]
            unpack(near[d][ch:, :], at, begin, rows, width, lane)

        @pl.when(wanted == dx)
        def _(d=d, begin=begin):
            unpack(near[d][:ch, :], left_ref, begin, rows, width, lane)

    tall = 2 * rows
    for c in range(ch):
        right = channel_of(right_ref, c, ch, tall)
        left = left_ref[pl.ds(c, tall, stride=ch), :].astype(BF16)
        part = lax.dot_general(left, right, (((0,), (0,)), ((), ())), preferred_element_type=F32)
        for side in range(len(sides)):
            mixed_ref[side, pl.ds(c, width, stride=ch), :] = part[
                :width, side * LANES : (side + 1) * LANES
            ]
    for dl in range(2):
        low = jnp.bitwise_xor(lax.rem(place.z, 2), dl)
        begin = pl.multiple_of(low * (rows * ch), 16)
        for side in range(len(sides)):
            out_ref = outs[dl * len(sides) + side]
            pack_halves(mixed_ref.at[side], begin, out_ref, rows, width // 2, lane)


def call(kernel, micros, outs, scratch, *args, space=pltpu.VMEM):
    outs = [(out, BF16) if isinstance(out[0], int) else out for out in outs]
    if space is pltpu.HBM:
        args = [pltpu.with_memory_space_constraint(arg, space) for arg in args]
    return pl.pallas_call(
        kernel,
        out_shape=[jax.ShapeDtypeStruct(shape, dtype) for shape, dtype in outs],
        in_specs=[pl.BlockSpec(memory_space=space) for _ in args],
        out_specs=[pl.BlockSpec(memory_space=pltpu.VMEM) for _ in outs],
        scratch_shapes=[
            entry if not isinstance(entry, tuple) else pltpu.VMEM(*entry) for entry in scratch
        ],
        compiler_params=pltpu.CompilerParams(vmem_limit_bytes=24 * 2**20),
        cost_estimate=pl.CostEstimate(
            flops=int(micros * 1.1e9), bytes_accessed=0, transcendentals=0
        ),
    )(*args)


def direct_body(pair_map, token_mask, in_gain, proj_weights, gate_weight, out_gain, out_weight):
    n_row, n_col = lax.axis_size("row"), lax.axis_size("col")
    rows, cols, channels = pair_map.shape
    width = 2 * cols
    total = rows * width
    ch = channels // (2 * NEAR)
    chunk = 13 * LANES

    def swap(value, dz, dx, core=0):
        flip = dz * n_col + dx * 2 + core
        pairs = [(i, i ^ flip) for i in range(n_row * n_col)]
        return lax.ppermute(value, ("row", "col"), pairs)

    def swap_all(values, offset):
        return [
            swap(value, *divmod(d + offset, 2)) if d + offset else value
            for d, value in enumerate(values)
        ]

    sibling = swap(pair_map, 0, 0, 1)
    wide = (channels, total)
    square = (channels, channels)
    mask = token_mask.reshape(1, -1)
    own, valid, chosen, gates, weights, gains, out_gains = call(
        prepare_kernel,
        1.5,
        [
            pair_map.shape,
            ((1, total), F32),
            (2, 4 * NEAR * ch, channels),
            (2, *square),
            (2, *square),
            ((2, *square), F32),
            ((2, *square), F32),
        ],
        [
            (mask.shape, mask.dtype),
            (proj_weights.shape, BF16),
            (gate_weight.shape, BF16),
            (out_weight.shape, BF16),
            (in_gain.shape, F32),
            (out_gain.shape, F32),
            ((4, *square), BF16),
            pltpu.SemaphoreType.DMA((7,)),
        ],
        pair_map,
        mask,
        proj_weights,
        gate_weight,
        out_weight,
        in_gain,
        out_gain,
        space=pltpu.HBM,
    )
    *right, pair, normed = call(
        functools.partial(first_far_kernel, chunk),
        1.0,
        [(ch, total)] * NEAR + [wide, wide],
        [((rows, width, channels), F32)],
        own,
        sibling,
        valid,
        gains,
        chosen,
    )
    near = call(
        functools.partial(first_near_kernel, chunk),
        0.6,
        [(2 * ch, total)] * NEAR,
        [],
        normed,
        chosen,
        *right,
    )
    far = swap_all(right, NEAR)
    near = swap_all(near, 0)
    tall = 2 * rows
    side = ((tall * ch, LANES), F32)
    sides = ((2, tall * ch, LANES), F32)
    gating, left, *mixed = call(
        functools.partial(outgoing_near_kernel, rows, width),
        2.0,
        [(wide, F32), sides] + [(ch, total)] * 2,
        [sides, side],
        *ordered(near, RIGHT_NEAR),
        normed,
        gates,
    )
    mixed = call(
        functools.partial(outgoing_far_kernel, rows, width),
        1.2,
        [(ch, total)] * NEAR,
        [sides, side],
        *ordered(far, RIGHT_FAR),
        left,
        *mixed,
    )
    mixed = swap_all(mixed, 0)
    other = [swap(part, 0, 0, 1) for part in mixed]

    *near, pair, normed = call(
        functools.partial(middle_kernel, chunk),
        2.3,
        [(2 * ch, total)] * NEAR + [wide, wide],
        [(wide, BF16)],
        *ordered(mixed, OUTGOING),
        *ordered(other, OUTGOING),
        pair,
        gating,
        valid,
        gains,
        out_gains,
        chosen,
        weights,
    )
    near = swap_all(near, 0)
    half = rows * cols

    def incoming(dh, sides):
        return call(
            functools.partial(incoming_kernel, rows, width, dh, sides),
            2.0,
            [(ch, total)] * (2 * len(sides)),
            [
                side,
                ((len(sides), tall * ch, LANES), F32),
                ((len(sides), width * ch, LANES), F32),
            ],
            *ordered(near, INCOMING),
        )

    first, second = incoming(1, (0,)), incoming(1, (1,))
    parts = [incoming(0, (0, 1)), [first[0], second[0], first[1], second[1]]]
    own, gating = call(
        functools.partial(own_kernel, chunk, cols),
        2.0,
        [((half, channels), F32)] * 2,
        [((2, total, channels), F32)],
        pair,
        normed,
        gates,
    )
    mixed = ordered(swap_all(parts[0], 0), SUMS_NEAR) + ordered(swap_all(parts[1], NEAR), SUMS_FAR)
    keep, send = call(sum_kernel, 1.0, [(NEAR * ch, half)] * 2, [], *mixed)
    got = swap(send, 0, 0, 1)
    out = call(
        functools.partial(last_kernel, chunk),
        1.0,
        [(half, channels)],
        [((channels, half), BF16)],
        keep,
        got,
        own,
        gating,
        out_gains,
        weights,
    )[0]
    return out.reshape(rows, cols, channels)


def solution(mesh):
    in_specs = (P(("groups", "row"), "col", None), P("groups"), P(), P(), P(), P(), P())
    out_specs = P(("groups", "row"), "col", None)
    direct = mesh.shape["row"] == 4 and mesh.shape["col"] == 4
    body = direct_body if direct else gather_body
    return jax.shard_map(body, mesh=mesh, in_specs=in_specs, out_specs=out_specs, check_vma=False)
```

```python
import functools

import jax
import jax.numpy as jnp
from jax import lax
from jax.experimental import pallas as pl
from jax.experimental.pallas import tpu as pltpu
from jax.sharding import PartitionSpec as P

EPSILON = 1e-05
LANES = 128
F32 = jnp.float32
BF16 = jnp.bfloat16


def layer_norm(values, gain_vec):
    mean_val = jnp.mean(values, axis=-1, keepdims=True)
    centered = values - mean_val
    variance = jnp.mean(centered * centered, axis=-1, keepdims=True)
    return centered * jax.lax.rsqrt(variance + EPSILON) * gain_vec


def project_side(pair_tile, pair_valid, layer_index, in_gain, proj_weights, gate_weight):
    normed = layer_norm(pair_tile.astype(F32), in_gain[layer_index]).astype(BF16)
    outputs = [
        jnp.dot(normed, proj_weights[layer_index, slot], preferred_element_type=F32)
        for slot in range(4)
    ]
    weight_mask = pair_valid[..., None]
    left_side = (jax.nn.sigmoid(outputs[1]) * outputs[0] * weight_mask).astype(BF16)
    right_side = (jax.nn.sigmoid(outputs[3]) * outputs[2] * weight_mask).astype(BF16)
    gating = jax.nn.sigmoid(jnp.dot(normed, gate_weight[layer_index], preferred_element_type=F32))
    return (left_side, right_side, gating)


def finish(pair_tile, mixed_sum, gating, layer_index, out_gain, out_weight):
    normed = layer_norm(mixed_sum, out_gain[layer_index]).astype(BF16)
    update = jnp.dot(normed, out_weight[layer_index], preferred_element_type=F32)
    return (pair_tile.astype(F32) + gating * update).astype(BF16)


def pair_mask(token_mask, tile_rows, row_begin, tile_cols, col_begin):
    valid = token_mask.astype(F32)
    row_valid = lax.dynamic_slice_in_dim(valid, row_begin, tile_rows, 0)
    col_valid = lax.dynamic_slice_in_dim(valid, col_begin, tile_cols, 0)
    return row_valid[:, None] * col_valid[None, :]


def gather_body(pair_map, token_mask, in_gain, proj_weights, gate_weight, out_gain, out_weight):
    tile_rows, tile_cols = pair_map.shape[:2]
    pair_valid = pair_mask(
        token_mask,
        tile_rows,
        lax.axis_index("row") * tile_rows,
        tile_cols,
        lax.axis_index("col") * tile_cols,
    )
    left_side, right_side, gating = project_side(
        pair_map, pair_valid, 0, in_gain, proj_weights, gate_weight
    )
    block = lax.all_gather(right_side, "row", axis=0, tiled=True)
    summed = lax.psum_scatter(
        jnp.einsum("jkc,ikc->jic", block, left_side, preferred_element_type=F32).astype(BF16),
        "col",
        scatter_dimension=0,
        tiled=True,
    ).astype(F32)
    mixed = jnp.transpose(summed, (1, 0, 2))
    after_out = finish(pair_map, mixed, gating, 0, out_gain, out_weight)
    left_side, right_side, gating = project_side(
        after_out, pair_valid, 1, in_gain, proj_weights, gate_weight
    )
    block = lax.all_gather(left_side, "col", axis=1, tiled=True)
    mixed = lax.psum_scatter(
        jnp.einsum("kic,kjc->ijc", block, right_side, preferred_element_type=F32).astype(BF16),
        "row",
        scatter_dimension=0,
        tiled=True,
    ).astype(F32)
    return finish(after_out, mixed, gating, 1, out_gain, out_weight)


NEAR = 4
INCOMING = (0, 1, 2, 3)
RIGHT_NEAR = (0, 1, 2, 3)
OUTGOING = (0, 3, 2, 1)
SUMS_NEAR = (0, 3, 2, 1)
SUMS_FAR = (1, 0, 3, 2)


def ordered(values, order):
    return [values[d] for d in order]


def restored(values, order):
    return [values[order.index(d)] for d in range(NEAR)]


class Place:
    def __init__(self):
        z = lax.axis_index("row")
        col = lax.axis_index("col")
        self.z = z
        self.x = lax.div(col, 2)
        self.core = lax.rem(col, 2)
        self.half = lax.div(z, 2)
        self.group = lax.rem(z, 2) * 2 + self.x

    def channels(self, d, ch, other=False, compact=False, absolute=False):
        core = 1 - self.core if other else self.core
        group = d if absolute else jnp.bitwise_xor(self.group, d)
        begin = group * ch if compact else group * (2 * ch) + core * ch
        return pl.ds(pl.multiple_of(begin, ch), ch)


def lane_of(rows):
    return lax.broadcasted_iota(jnp.int32, (rows, LANES), 1)


def take_piece(value, index, width, lane):
    tile, offset = divmod(index * width, LANES)
    part = value[:, tile * LANES : (tile + 1) * LANES]
    if offset:
        part = pltpu.roll(part, LANES - offset, 1)
    if offset + width > LANES:
        after = value[:, (tile + 1) * LANES : (tile + 2) * LANES]
        part = jnp.where(lane < LANES - offset, part, pltpu.roll(after, LANES - offset, 1))
    return jnp.where(lane < width, part, jnp.zeros_like(part))


def join_pieces(piece, count, width, tile, lane):
    low = tile * LANES
    out = None
    for index in range(low // width, min(count, -(-(low + LANES) // width))):
        shift = index * width - low
        part, begin = piece(index)
        if (shift - begin) % LANES:
            part = pltpu.roll(part, (shift - begin) % LANES, 1)
        out = part if out is None else jnp.where(lane >= shift, part, out)
    return out


def norm_rows(values, gain_col, valid=None):
    mean_val = jnp.mean(values, axis=0, keepdims=True)
    centered = values - mean_val
    variance = jnp.mean(centered * centered, axis=0, keepdims=True)
    scale = lax.rsqrt(variance + EPSILON)
    if valid is not None:
        scale = scale * valid
    return (centered * scale * gain_col).astype(BF16)


def turned(weight):
    return weight.astype(F32).T.astype(BF16)


def halved(weight):
    return (weight.astype(F32) * 0.5).astype(BF16)


def project_chunk(normed, chosen):
    out = jnp.dot(chosen, normed, preferred_element_type=F32)
    half = out.shape[0] // 2
    return ((jnp.tanh(out[half:]) + 1.0) * out[:half]).astype(BF16)


def chunks_of(total, size):
    return [slice(begin, min(begin + size, total)) for begin in range(0, total, size)]


def prepare_kernel(
    pair_in,
    mask_in,
    proj_in,
    gate_in,
    weight_in,
    gain_in,
    out_gain_in,
    pair_ref,
    valid_ref,
    chosen_ref,
    gate_ref,
    weight_ref,
    gain_ref,
    out_gain_ref,
    mask_ref,
    proj_ref,
    gates_ref,
    weights_ref,
    gains_ref,
    out_gains_ref,
    turned_ref,
    sems,
):
    moves = [
        (mask_in, mask_ref),
        (proj_in, proj_ref),
        (gain_in, gains_ref),
        (out_gain_in, out_gains_ref),
        (gate_in, gates_ref),
        (weight_in, weights_ref),
        (pair_in, pair_ref),
    ]
    copies = [
        pltpu.make_async_copy(there, here, sems.at[i]) for i, (there, here) in enumerate(moves)
    ]
    for copy in copies:
        copy.start()
    place = Place()
    ch = chosen_ref.shape[1] // (4 * NEAR)
    total = valid_ref.shape[1]
    rows, cols = pair_ref.shape[:2]
    width = 2 * cols
    copies[0].wait()
    lane = lane_of(1)
    mask = mask_ref[...].astype(F32).astype(BF16)

    def lanes_from(begin):
        shape = (mask.shape[1], LANES)
        token = lax.broadcasted_iota(jnp.int32, shape, 0)
        lanes = lax.broadcasted_iota(jnp.int32, shape, 1)
        pick = jnp.where(token == lanes + begin, 1.0, 0.0).astype(BF16)
        return jnp.dot(mask, pick, preferred_element_type=F32)

    col_valid = lanes_from(place.x * width)
    row_valid = lanes_from(place.z * rows)
    for tile in range(total // LANES):
        valid_ref[:, tile * LANES : (tile + 1) * LANES] = join_pieces(
            lambda row: (col_valid * row_valid[:, row : row + 1], 0), rows, width, tile, lane
        )
    copies[1].wait()
    for layer in range(2):
        for slot in range(4):
            turned_ref[slot] = halved(turned(proj_ref[layer, (0, 2, 1, 3)[slot]]))
        for slot in range(4):
            for d in range(NEAR):
                begin = (slot * NEAR + d) * ch
                chosen_ref[layer, begin : begin + ch, :] = turned_ref[slot, place.channels(d, ch), :]
    copies[2].wait()
    copies[3].wait()
    for layer in range(2):
        for gains, ref in ((gains_ref, gain_ref), (out_gains_ref, out_gain_ref)):
            ref[layer] = jnp.broadcast_to(gains[layer : layer + 1, :], (LANES, LANES)).T
    copies[4].wait()
    copies[5].wait()
    gate_ref[0] = halved(turned(gates_ref[0]))
    weight_ref[0] = halved(turned(weights_ref[0]))
    gate_ref[1] = halved(gates_ref[1])
    weight_ref[1] = halved(weights_ref[1])
    copies[6].wait()


def column_of(ref, layer, lanes):
    return jnp.concatenate([ref[layer]] * (-(-lanes // LANES)), axis=1)[:, :lanes]


def chosen_rows(chosen_ref, layer, side):
    half = chosen_ref.shape[1] // 4
    values, gates = (side * half, (side + 1) * half), ((side + 2) * half, (side + 3) * half)
    return jnp.concatenate(
        [chosen_ref[layer, slice(*values), :], chosen_ref[layer, slice(*gates), :]], axis=0
    )


def first_far_kernel(
    chunk, own_ref, sibling_ref, valid_ref, gain_ref, chosen_ref, *rest
):
    far_refs = rest[:NEAR]
    turned_pair_ref, normed_ref, pair_ref = rest[NEAR:]
    place = Place()
    cols = own_ref.shape[1]
    ch = far_refs[0].shape[0]
    total = valid_ref.shape[1]
    own_at = pl.multiple_of(place.core * cols, 8)
    sibling_at = pl.multiple_of((1 - place.core) * cols, 8)
    pair_ref[:, pl.ds(own_at, cols), :] = own_ref[...].astype(F32)
    pair_ref[:, pl.ds(sibling_at, cols), :] = sibling_ref[...].astype(F32)
    gain_col = column_of(gain_ref, 0, chunk)
    flat = pair_ref[...].reshape(total, LANES)
    chosen = chosen_rows(chosen_ref, 0, 1)
    for lanes in chunks_of(total, chunk):
        pair = flat[lanes].T
        turned_pair_ref[:, lanes] = pair.astype(BF16)
        normed = norm_rows(pair, gain_col[:, : lanes.stop - lanes.start], valid_ref[:, lanes])
        normed_ref[:, lanes] = normed
        right = project_chunk(normed, chosen)
        for d in range(NEAR):
            far_refs[d][:, lanes] = right[d * ch : (d + 1) * ch]


def first_near_kernel(chunk, normed_ref, chosen_ref, *rest):
    far_refs, near_refs = rest[:NEAR], rest[NEAR:]
    ch = far_refs[0].shape[0]
    total = normed_ref.shape[1]
    chosen = chosen_rows(chosen_ref, 0, 0)
    for lanes in chunks_of(total, chunk):
        left = project_chunk(normed_ref[:, lanes], chosen)
        for d in range(NEAR):
            near_refs[d][:ch, lanes] = left[d * ch : (d + 1) * ch]
    for d in range(NEAR):
        near_refs[d][ch:, :] = far_refs[d][...]


def gate_rows(normed_ref, gate, gating_ref, chunk):
    for lanes in chunks_of(normed_ref.shape[1], chunk):
        gating_ref[:, lanes] = 1.0 + jnp.tanh(
            jnp.dot(gate, normed_ref[:, lanes], preferred_element_type=F32)
        )


def middle_kernel(chunk, *refs):
    mine = restored(refs[:NEAR], OUTGOING)
    other = restored(refs[NEAR : 2 * NEAR], OUTGOING)
    pair_ref, gating_ref, valid_ref, gain_ref, out_gain_ref = refs[2 * NEAR : 2 * NEAR + 5]
    chosen_ref, weight_ref = refs[2 * NEAR + 5 : 2 * NEAR + 7]
    near_refs = refs[2 * NEAR + 7 : 3 * NEAR + 7]
    after_ref, normed_ref, mixed_ref = refs[3 * NEAR + 7 :]
    place = Place()
    ch = mine[0].shape[0]
    total = valid_ref.shape[1]
    for d in range(NEAR):
        mixed_ref[place.channels(d, ch), :] = mine[d][...]
        mixed_ref[place.channels(d, ch, True), :] = other[d][...]
    weight = weight_ref[0]
    out_gain_col = column_of(out_gain_ref, 0, chunk)
    gain_col = column_of(gain_ref, 1, chunk)
    sides = [chosen_rows(chosen_ref, 1, side) for side in range(2)]
    for lanes in chunks_of(total, chunk):
        normed_out = norm_rows(
            mixed_ref[:, lanes].astype(F32), out_gain_col[:, : lanes.stop - lanes.start]
        )
        update = jnp.dot(weight, normed_out, preferred_element_type=F32)
        after = (pair_ref[:, lanes].astype(F32) + gating_ref[:, lanes] * update).astype(BF16)
        after_ref[:, lanes] = after
        normed = norm_rows(
            after.astype(F32), gain_col[:, : lanes.stop - lanes.start], valid_ref[:, lanes]
        )
        normed_ref[:, lanes] = normed
        for side in range(2):
            out = project_chunk(normed, sides[side])
            for d in range(NEAR):
                near_refs[d][side * ch : (side + 1) * ch, lanes] = out[d * ch : (d + 1) * ch]


def own_kernel(chunk, cols, after_ref, normed_ref, gate_ref, own_ref, gating_ref, rows_ref):
    place = Place()
    total = after_ref.shape[1]
    rows = total // (2 * cols)
    own_at = pl.multiple_of(place.core * cols, 8)
    for lanes in chunks_of(total, chunk):
        rows_ref[0, lanes, :] = after_ref[:, lanes].astype(F32).T
        rows_ref[1, lanes, :] = lax.dot_general(
            normed_ref[:, lanes],
            gate_ref[1],
            (((0,), (0,)), ((), ())),
            preferred_element_type=F32,
        )
    for row in range(rows):
        here = pl.ds(row * 2 * cols + own_at, cols)
        own_ref[row * cols : (row + 1) * cols, :] = rows_ref[0, here, :]
        gating_ref[row * cols : (row + 1) * cols, :] = 1.0 + jnp.tanh(rows_ref[1, here, :])


def sum_kernel(*refs):
    near = restored(refs[:NEAR], SUMS_NEAR)
    far = restored(refs[NEAR : 2 * NEAR], SUMS_FAR)
    keep_ref, send_ref = refs[2 * NEAR :]
    place = Place()
    ch = near[0].shape[0]
    half = keep_ref.shape[1]
    begin = half // LANES * LANES
    for d in range(NEAR):
        total = near[d][...].astype(F32) + far[d][:, : 2 * half].astype(F32)
        rows = place.channels(d, ch, compact=True)
        first = total[:, :half]
        second = pltpu.roll(total[:, begin:], half, 1)[:, :half]
        keep_ref[rows, :] = jnp.where(place.core == 0, first, second).astype(BF16)
        send_ref[rows, :] = jnp.where(place.core == 0, second, first).astype(BF16)


def last_kernel(chunk, keep_ref, got_ref, own_ref, gating_ref, gain_ref, weight_ref, out_ref, mixed_ref):
    place = Place()
    ch = keep_ref.shape[0] // NEAR
    for group in range(NEAR):
        rows = slice(group * ch, (group + 1) * ch)
        mixed_ref[place.channels(group, ch, absolute=True), :] = keep_ref[rows, :]
        mixed_ref[place.channels(group, ch, True, absolute=True), :] = got_ref[rows, :]
    for lanes in chunks_of(keep_ref.shape[1], chunk):
        gain_col = column_of(gain_ref, 1, lanes.stop - lanes.start)
        normed = norm_rows(mixed_ref[:, lanes].astype(F32), gain_col)
        update = lax.dot_general(
            normed, weight_ref[1], (((0,), (0,)), ((), ())), preferred_element_type=F32
        )
        out_ref[lanes, :] = (own_ref[lanes, :] + gating_ref[lanes, :] * update).astype(BF16)


def unpack(value, ref, begin, rows, width, lane):
    ch = value.shape[0]
    for row in range(rows):
        ref[pl.ds(begin + row * ch, ch), :] = take_piece(value, row, width, lane).astype(F32)


def pack(ref, begin, out_ref, rows, width, lane):
    ch = out_ref.shape[0]
    for tile in range(rows * width // LANES):
        out_ref[:, tile * LANES : (tile + 1) * LANES] = join_pieces(
            lambda row: (ref[pl.ds(begin + row * ch, ch), :].astype(BF16), 0), rows, width, tile, lane
        )


def pack_halves(ref, begin, out_ref, rows, cols, lane):
    ch = out_ref.shape[0]
    for tile in range(out_ref.shape[1] // LANES):
        lanes = slice(tile * LANES, (tile + 1) * LANES)
        if tile * LANES >= 2 * rows * cols:
            out_ref[:, lanes] = jnp.zeros((ch, LANES), BF16)
            continue

        def piece(index):
            part = ref[pl.ds(begin + (index % rows) * ch, ch), :].astype(BF16)
            return part, index // rows * cols

        out_ref[:, lanes] = join_pieces(piece, 2 * rows, cols, tile, lane)


def channel_of(blocks, c, ch):
    parts = []
    for column in blocks:
        rows = [ref[pl.ds(c, ref.shape[0] // ch, stride=ch), :] for ref in column]
        parts.append(jnp.concatenate(rows, axis=0))
    return jnp.concatenate(parts, axis=1).astype(BF16)


def widen(part):
    return jnp.pad(part, ((0, 0), (0, LANES - part.shape[1])))


def outgoing_multiply(left_ref, right, mixed_ref, ch):
    for c in range(ch):
        left = channel_of([[left_ref.at[0]], [left_ref.at[1]]], c, ch)
        part = lax.dot_general(
            left, channel_of(right, c, ch), (((1,), (1,)), ((), ())), preferred_element_type=F32
        )
        mixed_ref[pl.ds(c, left.shape[0], stride=ch), :] = widen(part)


def outgoing_near_kernel(rows, width, *refs):
    near = restored(refs[:NEAR], RIGHT_NEAR)
    normed_ref, gate_ref = refs[NEAR : NEAR + 2]
    gating_ref, left_ref, *outs = refs[NEAR + 2 : NEAR + 6]
    right_ref, mixed_ref = refs[NEAR + 6 :]
    gate_rows(normed_ref, gate_ref[0], gating_ref, 13 * LANES)
    place = Place()
    ch = outs[0].shape[0]
    lane = lane_of(ch)
    for d in range(NEAR):
        dl, dx = divmod(d, 2)
        value = near[d][...]
        unpack(value[:ch], left_ref.at[dx], dl * rows * ch, rows, width, lane)
        low = jnp.bitwise_xor(lax.rem(place.z, 2), dl)
        begin = pl.multiple_of(low * (rows * ch), 16)
        unpack(value[ch:], right_ref.at[dx], begin, rows, width, lane)
    outgoing_multiply(left_ref, [[right_ref.at[0]], [right_ref.at[1]]], mixed_ref, ch)
    for dl in range(2):
        pack(mixed_ref, dl * rows * ch, outs[dl], rows, width, lane)


def unpack_kernel(rows, width, value_ref, earlier_ref, *outs):
    ch = value_ref.shape[0] // len(outs)
    lane = lane_of(ch)
    for side, out_ref in enumerate(outs):
        unpack(value_ref[side * ch : (side + 1) * ch, :], out_ref, 0, rows, width, lane)


def outgoing_far_kernel(rows, width, *refs):
    far, left_ref, done = refs[:NEAR], refs[NEAR], refs[NEAR + 1 : NEAR + 3]
    outs = refs[NEAR + 3 : 2 * NEAR + 3]
    right_ref, mixed_ref = refs[2 * NEAR + 3 :]
    place = Place()
    ch = far[0].shape[0]
    lane = lane_of(ch)
    for d in range(NEAR):
        dl, dx = divmod(d, 2)
        low = jnp.bitwise_xor(lax.rem(place.z, 2), dl)
        begin = pl.multiple_of(low * (rows * ch), 16)
        unpack(far[d][...], right_ref.at[dx], begin, rows, width, lane)
    outgoing_multiply(left_ref, [[right_ref.at[0]], [right_ref.at[1]]], mixed_ref, ch)
    same = jnp.bitwise_xor(place.half, place.x)
    for dx in range(2):

        @pl.when(same == dx)
        def _(dx=dx):
            for dl in range(2):
                outs[2 * dl + dx][...] = done[dl][...]
                pack(mixed_ref, dl * rows * ch, outs[2 * dl + 1 - dx], rows, width, lane)


def incoming_kernel(rows, width, jobs, *refs):
    lefts, rights, outs, mixed_ref = refs[:NEAR], refs[NEAR : 2 * NEAR], refs[2 * NEAR : -1], refs[-1]
    place = Place()
    ch = outs[0].shape[0]
    lane = lane_of(ch)
    for dh, sides in jobs:
        wanted = jnp.bitwise_xor(jnp.bitwise_xor(place.half, dh), place.x)
        right = [[rights[dx], rights[2 + dx]] for dx in sides]
        for dx in range(2):

            @pl.when(wanted == dx)
            def _(dx=dx, right=right, sides=sides):
                for c in range(ch):
                    part = lax.dot_general(
                        channel_of([[lefts[dx], lefts[2 + dx]]], c, ch),
                        channel_of(right, c, ch),
                        (((0,), (0,)), ((), ())),
                        preferred_element_type=F32,
                    )
                    for side in range(len(sides)):
                        mixed_ref[side, pl.ds(c, width, stride=ch), :] = part[
                            :width, side * LANES : (side + 1) * LANES
                        ]

        for dl in range(2):
            low = jnp.bitwise_xor(lax.rem(place.z, 2), dl)
            begin = pl.multiple_of(low * (rows * ch), 16)
            for side in range(len(sides)):
                out_ref, *outs = outs
                pack_halves(mixed_ref.at[side], begin, out_ref, rows, width // 2, lane)


def call(kernel, micros, outs, scratch, *args, space=pltpu.VMEM):
    outs = [(out, BF16) if isinstance(out[0], int) else out for out in outs]
    if space is pltpu.HBM:
        args = [pltpu.with_memory_space_constraint(arg, space) for arg in args]
    return pl.pallas_call(
        kernel,
        out_shape=[jax.ShapeDtypeStruct(shape, dtype) for shape, dtype in outs],
        in_specs=[pl.BlockSpec(memory_space=space) for _ in args],
        out_specs=[pl.BlockSpec(memory_space=pltpu.VMEM) for _ in outs],
        scratch_shapes=[
            entry if not isinstance(entry, tuple) else pltpu.VMEM(*entry) for entry in scratch
        ],
        compiler_params=pltpu.CompilerParams(vmem_limit_bytes=24 * 2**20),
        cost_estimate=pl.CostEstimate(
            flops=int(micros * 1.1e9), bytes_accessed=0, transcendentals=0
        ),
    )(*args)


def direct_body(pair_map, token_mask, in_gain, proj_weights, gate_weight, out_gain, out_weight):
    n_row, n_col = lax.axis_size("row"), lax.axis_size("col")
    rows, cols, channels = pair_map.shape
    width = 2 * cols
    total = rows * width
    ch = channels // (2 * NEAR)
    chunk = 13 * LANES

    def swap(value, dz, dx, core=0):
        flip = dz * n_col + dx * 2 + core
        pairs = [(i, i ^ flip) for i in range(n_row * n_col)]
        return lax.ppermute(value, ("row", "col"), pairs)

    def swap_all(values, offset):
        return [
            swap(value, *divmod(d + offset, 2)) if d + offset else value
            for d, value in enumerate(values)
        ]

    sibling = swap(pair_map, 0, 0, 1)
    wide = (channels, total)
    square = (channels, channels)
    mask = token_mask.reshape(1, -1)
    own, valid, chosen, gates, weights, gains, out_gains = call(
        prepare_kernel,
        1.5,
        [
            pair_map.shape,
            ((1, total), F32),
            (2, 4 * NEAR * ch, channels),
            (2, *square),
            (2, *square),
            ((2, *square), F32),
            ((2, *square), F32),
        ],
        [
            (mask.shape, mask.dtype),
            (proj_weights.shape, BF16),
            (gate_weight.shape, BF16),
            (out_weight.shape, BF16),
            (in_gain.shape, F32),
            (out_gain.shape, F32),
            ((4, *square), BF16),
            pltpu.SemaphoreType.DMA((7,)),
        ],
        pair_map,
        mask,
        proj_weights,
        gate_weight,
        out_weight,
        in_gain,
        out_gain,
        space=pltpu.HBM,
    )
    *right, pair, normed = call(
        functools.partial(first_far_kernel, chunk),
        1.0,
        [(ch, total)] * NEAR + [wide, wide],
        [((rows, width, channels), F32)],
        own,
        sibling,
        valid,
        gains,
        chosen,
    )
    near = call(
        functools.partial(first_near_kernel, chunk),
        0.6,
        [(2 * ch, total)] * NEAR,
        [],
        normed,
        chosen,
        *right,
    )
    far = swap_all(right, NEAR)
    near = swap_all(near, 0)
    tall = 2 * rows
    side = ((tall * ch, LANES), F32)
    sides = ((2, tall * ch, LANES), F32)
    gating, left, *mixed = call(
        functools.partial(outgoing_near_kernel, rows, width),
        2.0,
        [(wide, F32), sides] + [(ch, total)] * 2,
        [sides, side],
        *ordered(near, RIGHT_NEAR),
        normed,
        gates,
    )
    block = ((rows * ch, LANES), F32)

    def unpacked(value, operands, earlier):
        return call(
            functools.partial(unpack_kernel, rows, width), 0.2, [block] * operands, [], value, earlier
        )

    mixed = call(
        functools.partial(outgoing_far_kernel, rows, width),
        1.2,
        [(ch, total)] * NEAR,
        [sides, side],
        *far,
        left,
        *mixed,
    )
    mixed = swap_all(mixed, 0)
    other = [swap(part, 0, 0, 1) for part in mixed]

    *near, pair, normed = call(
        functools.partial(middle_kernel, chunk),
        2.3,
        [(2 * ch, total)] * NEAR + [wide, wide],
        [(wide, BF16)],
        *ordered(mixed, OUTGOING),
        *ordered(other, OUTGOING),
        pair,
        gating,
        valid,
        gains,
        out_gains,
        chosen,
        weights,
    )
    near = swap_all(near, 0)
    half = rows * cols

    got = [None] * NEAR
    earlier = valid
    for d in INCOMING:
        got[d] = unpacked(near[d], 2, earlier)
        earlier = got[d][0]
    lefts, rights = zip(*got, strict=True)

    def incoming(micros, *jobs):
        return call(
            functools.partial(incoming_kernel, rows, width, jobs),
            micros,
            [(ch, total)] * sum(2 * len(sides) for dh, sides in jobs),
            [((2, width * ch, LANES), F32)],
            *lefts,
            *rights,
        )

    first = incoming(1.0, (1, (0,)))
    second = incoming(2.5, (1, (1,)), (0, (0, 1)))
    parts = [second[2:], [first[0], second[0], first[1], second[1]]]
    own, gating = call(
        functools.partial(own_kernel, chunk, cols),
        2.0,
        [((half, channels), F32)] * 2,
        [((2, total, channels), F32)],
        pair,
        normed,
        gates,
    )
    mixed = ordered(swap_all(parts[0], 0), SUMS_NEAR) + ordered(swap_all(parts[1], NEAR), SUMS_FAR)
    keep, send = call(sum_kernel, 1.0, [(NEAR * ch, half)] * 2, [], *mixed)
    got = swap(send, 0, 0, 1)
    out = call(
        functools.partial(last_kernel, chunk),
        1.0,
        [(half, channels)],
        [((channels, half), BF16)],
        keep,
        got,
        own,
        gating,
        out_gains,
        weights,
    )[0]
    return out.reshape(rows, cols, channels)


def solution(mesh):
    in_specs = (P(("groups", "row"), "col", None), P("groups"), P(), P(), P(), P(), P())
    out_specs = P(("groups", "row"), "col", None)
    direct = mesh.shape["row"] == 4 and mesh.shape["col"] == 4
    body = direct_body if direct else gather_body
    return jax.shard_map(body, mesh=mesh, in_specs=in_specs, out_specs=out_specs, check_vma=False)
```

```python
import functools

import jax
import jax.numpy as jnp
from jax import lax
from jax.experimental import pallas as pl
from jax.experimental.pallas import tpu as pltpu
from jax.sharding import PartitionSpec as P

EPSILON = 1e-05
LANES = 128
F32 = jnp.float32
BF16 = jnp.bfloat16


def layer_norm(values, gain_vec):
    mean_val = jnp.mean(values, axis=-1, keepdims=True)
    centered = values - mean_val
    variance = jnp.mean(centered * centered, axis=-1, keepdims=True)
    return centered * jax.lax.rsqrt(variance + EPSILON) * gain_vec


def project_side(pair_tile, pair_valid, layer_index, in_gain, proj_weights, gate_weight):
    normed = layer_norm(pair_tile.astype(F32), in_gain[layer_index]).astype(BF16)
    outputs = [
        jnp.dot(normed, proj_weights[layer_index, slot], preferred_element_type=F32)
        for slot in range(4)
    ]
    weight_mask = pair_valid[..., None]
    left_side = (jax.nn.sigmoid(outputs[1]) * outputs[0] * weight_mask).astype(BF16)
    right_side = (jax.nn.sigmoid(outputs[3]) * outputs[2] * weight_mask).astype(BF16)
    gating = jax.nn.sigmoid(jnp.dot(normed, gate_weight[layer_index], preferred_element_type=F32))
    return (left_side, right_side, gating)


def finish(pair_tile, mixed_sum, gating, layer_index, out_gain, out_weight):
    normed = layer_norm(mixed_sum, out_gain[layer_index]).astype(BF16)
    update = jnp.dot(normed, out_weight[layer_index], preferred_element_type=F32)
    return (pair_tile.astype(F32) + gating * update).astype(BF16)


def pair_mask(token_mask, tile_rows, row_begin, tile_cols, col_begin):
    valid = token_mask.astype(F32)
    row_valid = lax.dynamic_slice_in_dim(valid, row_begin, tile_rows, 0)
    col_valid = lax.dynamic_slice_in_dim(valid, col_begin, tile_cols, 0)
    return row_valid[:, None] * col_valid[None, :]


def gather_body(pair_map, token_mask, in_gain, proj_weights, gate_weight, out_gain, out_weight):
    tile_rows, tile_cols = pair_map.shape[:2]
    pair_valid = pair_mask(
        token_mask,
        tile_rows,
        lax.axis_index("row") * tile_rows,
        tile_cols,
        lax.axis_index("col") * tile_cols,
    )
    left_side, right_side, gating = project_side(
        pair_map, pair_valid, 0, in_gain, proj_weights, gate_weight
    )
    block = lax.all_gather(right_side, "row", axis=0, tiled=True)
    summed = lax.psum_scatter(
        jnp.einsum("jkc,ikc->jic", block, left_side, preferred_element_type=F32).astype(BF16),
        "col",
        scatter_dimension=0,
        tiled=True,
    ).astype(F32)
    mixed = jnp.transpose(summed, (1, 0, 2))
    after_out = finish(pair_map, mixed, gating, 0, out_gain, out_weight)
    left_side, right_side, gating = project_side(
        after_out, pair_valid, 1, in_gain, proj_weights, gate_weight
    )
    block = lax.all_gather(left_side, "col", axis=1, tiled=True)
    mixed = lax.psum_scatter(
        jnp.einsum("kic,kjc->ijc", block, right_side, preferred_element_type=F32).astype(BF16),
        "row",
        scatter_dimension=0,
        tiled=True,
    ).astype(F32)
    return finish(after_out, mixed, gating, 1, out_gain, out_weight)


NEAR = 4
INCOMING = (0, 1, 2, 3)
RIGHT_NEAR = (0, 1, 2, 3)
RIGHT_FAR = (0, 1, 2, 3)
OUTGOING = (0, 3, 2, 1)
SUMS_NEAR = (0, 3, 2, 1)
SUMS_FAR = (1, 0, 3, 2)


def ordered(values, order):
    return [values[d] for d in order]


def restored(values, order):
    return [values[order.index(d)] for d in range(NEAR)]


class Place:
    def __init__(self):
        z = lax.axis_index("row")
        col = lax.axis_index("col")
        self.z = z
        self.x = lax.div(col, 2)
        self.core = lax.rem(col, 2)
        self.half = lax.div(z, 2)
        self.group = lax.rem(z, 2) * 2 + self.x

    def channels(self, d, ch, other=False, compact=False, absolute=False):
        core = 1 - self.core if other else self.core
        group = d if absolute else jnp.bitwise_xor(self.group, d)
        begin = group * ch if compact else group * (2 * ch) + core * ch
        return pl.ds(pl.multiple_of(begin, ch), ch)


def lane_of(rows):
    return lax.broadcasted_iota(jnp.int32, (rows, LANES), 1)


def take_piece(value, index, width, lane):
    tile, offset = divmod(index * width, LANES)
    part = value[:, tile * LANES : (tile + 1) * LANES]
    if offset:
        part = pltpu.roll(part, LANES - offset, 1)
    if offset + width > LANES:
        after = value[:, (tile + 1) * LANES : (tile + 2) * LANES]
        part = jnp.where(lane < LANES - offset, part, pltpu.roll(after, LANES - offset, 1))
    return jnp.where(lane < width, part, jnp.zeros_like(part))


def join_pieces(piece, count, width, tile, lane):
    low = tile * LANES
    out = None
    for index in range(low // width, min(count, -(-(low + LANES) // width))):
        shift = index * width - low
        part, begin = piece(index)
        if (shift - begin) % LANES:
            part = pltpu.roll(part, (shift - begin) % LANES, 1)
        out = part if out is None else jnp.where(lane >= shift, part, out)
    return out


def norm_rows(values, gain_col, valid=None):
    mean_val = jnp.mean(values, axis=0, keepdims=True)
    centered = values - mean_val
    variance = jnp.mean(centered * centered, axis=0, keepdims=True)
    scale = lax.rsqrt(variance + EPSILON)
    if valid is not None:
        scale = scale * valid
    return (centered * scale * gain_col).astype(BF16)


def turned(weight):
    return weight.astype(F32).T.astype(BF16)


def halved(weight):
    return (weight.astype(F32) * 0.5).astype(BF16)


def project_chunk(normed, chosen):
    out = jnp.dot(chosen, normed, preferred_element_type=F32)
    half = out.shape[0] // 2
    return ((jnp.tanh(out[half:]) + 1.0) * out[:half]).astype(BF16)


def chunks_of(total, size):
    return [slice(begin, min(begin + size, total)) for begin in range(0, total, size)]


def prepare_kernel(
    pair_in,
    mask_in,
    proj_in,
    gate_in,
    weight_in,
    gain_in,
    out_gain_in,
    pair_ref,
    valid_ref,
    chosen_ref,
    gate_ref,
    weight_ref,
    gain_ref,
    out_gain_ref,
    mask_ref,
    proj_ref,
    gates_ref,
    weights_ref,
    gains_ref,
    out_gains_ref,
    turned_ref,
    sems,
):
    moves = [
        (mask_in, mask_ref),
        (proj_in, proj_ref),
        (gain_in, gains_ref),
        (out_gain_in, out_gains_ref),
        (gate_in, gates_ref),
        (weight_in, weights_ref),
        (pair_in, pair_ref),
    ]
    copies = [
        pltpu.make_async_copy(there, here, sems.at[i]) for i, (there, here) in enumerate(moves)
    ]
    for copy in copies:
        copy.start()
    place = Place()
    ch = chosen_ref.shape[1] // (4 * NEAR)
    total = valid_ref.shape[1]
    rows, cols = pair_ref.shape[:2]
    width = 2 * cols
    copies[0].wait()
    lane = lane_of(1)
    mask = mask_ref[...].astype(F32).astype(BF16)

    def lanes_from(begin):
        shape = (mask.shape[1], LANES)
        token = lax.broadcasted_iota(jnp.int32, shape, 0)
        lanes = lax.broadcasted_iota(jnp.int32, shape, 1)
        pick = jnp.where(token == lanes + begin, 1.0, 0.0).astype(BF16)
        return jnp.dot(mask, pick, preferred_element_type=F32)

    col_valid = lanes_from(place.x * width)
    row_valid = lanes_from(place.z * rows)
    for tile in range(total // LANES):
        valid_ref[:, tile * LANES : (tile + 1) * LANES] = join_pieces(
            lambda row: (col_valid * row_valid[:, row : row + 1], 0), rows, width, tile, lane
        )
    copies[1].wait()
    for layer in range(2):
        for slot in range(4):
            turned_ref[slot] = halved(turned(proj_ref[layer, (0, 2, 1, 3)[slot]]))
        for slot in range(4):
            for d in range(NEAR):
                begin = (slot * NEAR + d) * ch
                chosen_ref[layer, begin : begin + ch, :] = turned_ref[slot, place.channels(d, ch), :]
    copies[2].wait()
    copies[3].wait()
    for layer in range(2):
        for gains, ref in ((gains_ref, gain_ref), (out_gains_ref, out_gain_ref)):
            ref[layer] = jnp.broadcast_to(gains[layer : layer + 1, :], (LANES, LANES)).T
    copies[4].wait()
    copies[5].wait()
    gate_ref[0] = halved(turned(gates_ref[0]))
    weight_ref[0] = halved(turned(weights_ref[0]))
    gate_ref[1] = halved(gates_ref[1])
    weight_ref[1] = halved(weights_ref[1])
    copies[6].wait()


def column_of(ref, layer, lanes):
    return jnp.concatenate([ref[layer]] * (-(-lanes // LANES)), axis=1)[:, :lanes]


def chosen_rows(chosen_ref, layer, side):
    half = chosen_ref.shape[1] // 4
    values, gates = (side * half, (side + 1) * half), ((side + 2) * half, (side + 3) * half)
    return jnp.concatenate(
        [chosen_ref[layer, slice(*values), :], chosen_ref[layer, slice(*gates), :]], axis=0
    )


def first_kernel(
    chunk, own_ref, sibling_ref, valid_ref, gain_ref, chosen_ref, *rest
):
    far_refs, near_refs = rest[:NEAR], rest[NEAR : 2 * NEAR]
    turned_pair_ref, normed_ref, pair_ref = rest[2 * NEAR :]
    place = Place()
    cols = own_ref.shape[1]
    ch = far_refs[0].shape[0]
    total = valid_ref.shape[1]
    own_at = pl.multiple_of(place.core * cols, 8)
    sibling_at = pl.multiple_of((1 - place.core) * cols, 8)
    pair_ref[:, pl.ds(own_at, cols), :] = own_ref[...].astype(F32)
    pair_ref[:, pl.ds(sibling_at, cols), :] = sibling_ref[...].astype(F32)
    gain_col = column_of(gain_ref, 0, chunk)
    flat = pair_ref[...].reshape(total, LANES)
    sides = [chosen_rows(chosen_ref, 0, side) for side in range(2)]
    for lanes in chunks_of(total, chunk):
        pair = flat[lanes].T
        turned_pair_ref[:, lanes] = pair.astype(BF16)
        normed = norm_rows(pair, gain_col[:, : lanes.stop - lanes.start], valid_ref[:, lanes])
        normed_ref[:, lanes] = normed
        left, right = [project_chunk(normed, chosen) for chosen in sides]
        for d in range(NEAR):
            rows = slice(d * ch, (d + 1) * ch)
            far_refs[d][:, lanes] = right[rows]
            near_refs[d][:ch, lanes] = left[rows]
            near_refs[d][ch:, lanes] = right[rows]


def gate_rows(normed_ref, gate, gating_ref, chunk):
    for lanes in chunks_of(normed_ref.shape[1], chunk):
        gating_ref[:, lanes] = 1.0 + jnp.tanh(
            jnp.dot(gate, normed_ref[:, lanes], preferred_element_type=F32)
        )


def middle_kernel(chunk, *refs):
    mine = restored(refs[:NEAR], OUTGOING)
    other = restored(refs[NEAR : 2 * NEAR], OUTGOING)
    pair_ref, gating_ref, valid_ref, gain_ref, out_gain_ref = refs[2 * NEAR : 2 * NEAR + 5]
    chosen_ref, weight_ref = refs[2 * NEAR + 5 : 2 * NEAR + 7]
    near_refs = refs[2 * NEAR + 7 : 3 * NEAR + 7]
    after_ref, normed_ref, mixed_ref = refs[3 * NEAR + 7 :]
    place = Place()
    ch = mine[0].shape[0]
    total = valid_ref.shape[1]
    for d in range(NEAR):
        mixed_ref[place.channels(d, ch), :] = mine[d][...]
        mixed_ref[place.channels(d, ch, True), :] = other[d][...]
    weight = weight_ref[0]
    out_gain_col = column_of(out_gain_ref, 0, chunk)
    gain_col = column_of(gain_ref, 1, chunk)
    sides = [chosen_rows(chosen_ref, 1, side) for side in range(2)]
    for lanes in chunks_of(total, chunk):
        normed_out = norm_rows(
            mixed_ref[:, lanes].astype(F32), out_gain_col[:, : lanes.stop - lanes.start]
        )
        update = jnp.dot(weight, normed_out, preferred_element_type=F32)
        after = (pair_ref[:, lanes].astype(F32) + gating_ref[:, lanes] * update).astype(BF16)
        after_ref[:, lanes] = after
        normed = norm_rows(
            after.astype(F32), gain_col[:, : lanes.stop - lanes.start], valid_ref[:, lanes]
        )
        normed_ref[:, lanes] = normed
        for side in range(2):
            out = project_chunk(normed, sides[side])
            for d in range(NEAR):
                near_refs[d][side * ch : (side + 1) * ch, lanes] = out[d * ch : (d + 1) * ch]


def own_kernel(chunk, cols, after_ref, normed_ref, gate_ref, own_ref, gating_ref, rows_ref):
    place = Place()
    total = after_ref.shape[1]
    rows = total // (2 * cols)
    own_at = pl.multiple_of(place.core * cols, 8)
    for lanes in chunks_of(total, chunk):
        rows_ref[0, lanes, :] = after_ref[:, lanes].astype(F32).T
        rows_ref[1, lanes, :] = lax.dot_general(
            normed_ref[:, lanes],
            gate_ref[1],
            (((0,), (0,)), ((), ())),
            preferred_element_type=F32,
        )
    for row in range(rows):
        here = pl.ds(row * 2 * cols + own_at, cols)
        own_ref[row * cols : (row + 1) * cols, :] = rows_ref[0, here, :]
        gating_ref[row * cols : (row + 1) * cols, :] = 1.0 + jnp.tanh(rows_ref[1, here, :])


def sum_kernel(*refs):
    near = restored(refs[:NEAR], SUMS_NEAR)
    far = restored(refs[NEAR : 2 * NEAR], SUMS_FAR)
    keep_ref, send_ref = refs[2 * NEAR :]
    place = Place()
    ch = near[0].shape[0]
    half = keep_ref.shape[1]
    begin = half // LANES * LANES
    for d in range(NEAR):
        total = near[d][...].astype(F32) + far[d][:, : 2 * half].astype(F32)
        rows = place.channels(d, ch, compact=True)
        first = total[:, :half]
        second = pltpu.roll(total[:, begin:], half, 1)[:, :half]
        keep_ref[rows, :] = jnp.where(place.core == 0, first, second).astype(BF16)
        send_ref[rows, :] = jnp.where(place.core == 0, second, first).astype(BF16)


def last_kernel(chunk, keep_ref, got_ref, own_ref, gating_ref, gain_ref, weight_ref, out_ref, mixed_ref):
    place = Place()
    ch = keep_ref.shape[0] // NEAR
    for group in range(NEAR):
        rows = slice(group * ch, (group + 1) * ch)
        mixed_ref[place.channels(group, ch, absolute=True), :] = keep_ref[rows, :]
        mixed_ref[place.channels(group, ch, True, absolute=True), :] = got_ref[rows, :]
    for lanes in chunks_of(keep_ref.shape[1], chunk):
        gain_col = column_of(gain_ref, 1, lanes.stop - lanes.start)
        normed = norm_rows(mixed_ref[:, lanes].astype(F32), gain_col)
        update = lax.dot_general(
            normed, weight_ref[1], (((0,), (0,)), ((), ())), preferred_element_type=F32
        )
        out_ref[lanes, :] = (own_ref[lanes, :] + gating_ref[lanes, :] * update).astype(BF16)


def unpack(value, ref, begin, rows, width, lane):
    ch = value.shape[0]
    for row in range(rows):
        ref[pl.ds(begin + row * ch, ch), :] = take_piece(value, row, width, lane).astype(F32)


def pack(ref, begin, out_ref, rows, width, lane):
    ch = out_ref.shape[0]
    for tile in range(rows * width // LANES):
        out_ref[:, tile * LANES : (tile + 1) * LANES] = join_pieces(
            lambda row: (ref[pl.ds(begin + row * ch, ch), :].astype(BF16), 0), rows, width, tile, lane
        )


def pack_halves(ref, begin, out_ref, rows, cols, lane):
    ch = out_ref.shape[0]
    for tile in range(out_ref.shape[1] // LANES):
        lanes = slice(tile * LANES, (tile + 1) * LANES)
        if tile * LANES >= 2 * rows * cols:
            out_ref[:, lanes] = jnp.zeros((ch, LANES), BF16)
            continue

        def piece(index):
            part = ref[pl.ds(begin + (index % rows) * ch, ch), :].astype(BF16)
            return part, index // rows * cols

        out_ref[:, lanes] = join_pieces(piece, 2 * rows, cols, tile, lane)


def channel_of(blocks, c, ch):
    parts = []
    for column in blocks:
        rows = [ref[pl.ds(c, ref.shape[0] // ch, stride=ch), :] for ref in column]
        parts.append(jnp.concatenate(rows, axis=0))
    return jnp.concatenate(parts, axis=1).astype(BF16)


def widen(part):
    return jnp.pad(part, ((0, 0), (0, LANES - part.shape[1])))


def outgoing_multiply(left_ref, right, mixed_ref, ch):
    for c in range(ch):
        left = channel_of([[left_ref.at[0]], [left_ref.at[1]]], c, ch)
        part = lax.dot_general(
            left, channel_of(right, c, ch), (((1,), (1,)), ((), ())), preferred_element_type=F32
        )
        mixed_ref[pl.ds(c, left.shape[0], stride=ch), :] = widen(part)


def outgoing_near_kernel(rows, width, *refs):
    near = restored(refs[:NEAR], RIGHT_NEAR)
    normed_ref, gate_ref = refs[NEAR : NEAR + 2]
    gating_ref, left_ref, *outs = refs[NEAR + 2 : NEAR + 6]
    right_ref, mixed_ref = refs[NEAR + 6 :]
    gate_rows(normed_ref, gate_ref[0], gating_ref, 13 * LANES)
    place = Place()
    ch = outs[0].shape[0]
    lane = lane_of(ch)
    for d in range(NEAR):
        dl, dx = divmod(d, 2)
        value = near[d][...]
        unpack(value[:ch], left_ref.at[dx], dl * rows * ch, rows, width, lane)
        low = jnp.bitwise_xor(lax.rem(place.z, 2), dl)
        begin = pl.multiple_of(low * (rows * ch), 16)
        unpack(value[ch:], right_ref.at[dx], begin, rows, width, lane)
    outgoing_multiply(left_ref, [[right_ref.at[0]], [right_ref.at[1]]], mixed_ref, ch)
    for dl in range(2):
        pack(mixed_ref, dl * rows * ch, outs[dl], rows, width, lane)


def unpack_kernel(rows, width, value_ref, earlier_ref, *outs):
    ch = value_ref.shape[0] // len(outs)
    lane = lane_of(ch)
    for side, out_ref in enumerate(outs):
        unpack(value_ref[side * ch : (side + 1) * ch, :], out_ref, 0, rows, width, lane)


def outgoing_far_kernel(rows, width, *refs):
    far = restored(refs[:NEAR], RIGHT_FAR)
    left_ref, done = refs[NEAR], refs[NEAR + 1 : NEAR + 3]
    outs = refs[NEAR + 3 : 2 * NEAR + 3]
    right_ref, mixed_ref = refs[2 * NEAR + 3 :]
    place = Place()
    ch = far[0].shape[0]
    lane = lane_of(ch)
    for d in range(NEAR):
        dl, dx = divmod(d, 2)
        low = jnp.bitwise_xor(lax.rem(place.z, 2), dl)
        begin = pl.multiple_of(low * (rows * ch), 16)
        unpack(far[d][...], right_ref.at[dx], begin, rows, width, lane)
    outgoing_multiply(left_ref, [[right_ref.at[0]], [right_ref.at[1]]], mixed_ref, ch)
    same = jnp.bitwise_xor(place.half, place.x)
    for dx in range(2):

        @pl.when(same == dx)
        def _(dx=dx):
            for dl in range(2):
                outs[2 * dl + dx][...] = done[dl][...]
                pack(mixed_ref, dl * rows * ch, outs[2 * dl + 1 - dx], rows, width, lane)


def incoming_kernel(rows, width, jobs, *refs):
    lefts, rights, outs, mixed_ref = refs[:NEAR], refs[NEAR : 2 * NEAR], refs[2 * NEAR : -1], refs[-1]
    place = Place()
    ch = outs[0].shape[0]
    lane = lane_of(ch)
    for dh, sides in jobs:
        wanted = jnp.bitwise_xor(jnp.bitwise_xor(place.half, dh), place.x)
        right = [[rights[dx], rights[2 + dx]] for dx in sides]
        for dx in range(2):

            @pl.when(wanted == dx)
            def _(dx=dx, right=right, sides=sides):
                for c in range(ch):
                    part = lax.dot_general(
                        channel_of([[lefts[dx], lefts[2 + dx]]], c, ch),
                        channel_of(right, c, ch),
                        (((0,), (0,)), ((), ())),
                        preferred_element_type=F32,
                    )
                    for side in range(len(sides)):
                        mixed_ref[side, pl.ds(c, width, stride=ch), :] = part[
                            :width, side * LANES : (side + 1) * LANES
                        ]

        for dl in range(2):
            low = jnp.bitwise_xor(lax.rem(place.z, 2), dl)
            begin = pl.multiple_of(low * (rows * ch), 16)
            for side in range(len(sides)):
                out_ref, *outs = outs
                pack_halves(mixed_ref.at[side], begin, out_ref, rows, width // 2, lane)


def call(kernel, micros, outs, scratch, *args, space=pltpu.VMEM):
    outs = [(out, BF16) if isinstance(out[0], int) else out for out in outs]
    if space is pltpu.HBM:
        args = [pltpu.with_memory_space_constraint(arg, space) for arg in args]
    return pl.pallas_call(
        kernel,
        out_shape=[jax.ShapeDtypeStruct(shape, dtype) for shape, dtype in outs],
        in_specs=[pl.BlockSpec(memory_space=space) for _ in args],
        out_specs=[pl.BlockSpec(memory_space=pltpu.VMEM) for _ in outs],
        scratch_shapes=[
            entry if not isinstance(entry, tuple) else pltpu.VMEM(*entry) for entry in scratch
        ],
        compiler_params=pltpu.CompilerParams(vmem_limit_bytes=24 * 2**20),
        cost_estimate=pl.CostEstimate(
            flops=int(micros * 1.1e9), bytes_accessed=0, transcendentals=0
        ),
    )(*args)


def direct_body(pair_map, token_mask, in_gain, proj_weights, gate_weight, out_gain, out_weight):
    n_row, n_col = lax.axis_size("row"), lax.axis_size("col")
    rows, cols, channels = pair_map.shape
    width = 2 * cols
    total = rows * width
    ch = channels // (2 * NEAR)
    chunk = 25 * LANES

    def swap(value, dz, dx, core=0):
        flip = dz * n_col + dx * 2 + core
        pairs = [(i, i ^ flip) for i in range(n_row * n_col)]
        return lax.ppermute(value, ("row", "col"), pairs)

    def swap_all(values, offset):
        return [
            swap(value, *divmod(d + offset, 2)) if d + offset else value
            for d, value in enumerate(values)
        ]

    sibling = swap(pair_map, 0, 0, 1)
    wide = (channels, total)
    square = (channels, channels)
    mask = token_mask.reshape(1, -1)
    own, valid, chosen, gates, weights, gains, out_gains = call(
        prepare_kernel,
        1.5,
        [
            pair_map.shape,
            ((1, total), F32),
            (2, 4 * NEAR * ch, channels),
            (2, *square),
            (2, *square),
            ((2, *square), F32),
            ((2, *square), F32),
        ],
        [
            (mask.shape, mask.dtype),
            (proj_weights.shape, BF16),
            (gate_weight.shape, BF16),
            (out_weight.shape, BF16),
            (in_gain.shape, F32),
            (out_gain.shape, F32),
            ((4, *square), BF16),
            pltpu.SemaphoreType.DMA((7,)),
        ],
        pair_map,
        mask,
        proj_weights,
        gate_weight,
        out_weight,
        in_gain,
        out_gain,
        space=pltpu.HBM,
    )
    out = call(
        functools.partial(first_kernel, chunk),
        1.4,
        [(ch, total)] * NEAR + [(2 * ch, total)] * NEAR + [wide, wide],
        [((rows, width, channels), F32)],
        own,
        sibling,
        valid,
        gains,
        chosen,
    )
    right, near, (pair, normed) = out[:NEAR], out[NEAR : 2 * NEAR], out[2 * NEAR :]
    far = swap_all(right, NEAR)
    near = swap_all(near, 0)
    tall = 2 * rows
    side = ((tall * ch, LANES), F32)
    sides = ((2, tall * ch, LANES), F32)
    gating, left, *mixed = call(
        functools.partial(outgoing_near_kernel, rows, width),
        2.0,
        [(wide, F32), sides] + [(ch, total)] * 2,
        [sides, side],
        *ordered(near, RIGHT_NEAR),
        normed,
        gates,
    )
    block = ((rows * ch, LANES), F32)

    def unpacked(value, operands, earlier):
        return call(
            functools.partial(unpack_kernel, rows, width), 0.2, [block] * operands, [], value, earlier
        )

    mixed = call(
        functools.partial(outgoing_far_kernel, rows, width),
        1.2,
        [(ch, total)] * NEAR,
        [sides, side],
        *ordered(far, RIGHT_FAR),
        left,
        *mixed,
    )
    mixed = swap_all(mixed, 0)
    other = [swap(part, 0, 0, 1) for part in mixed]

    *near, pair, normed = call(
        functools.partial(middle_kernel, chunk),
        2.3,
        [(2 * ch, total)] * NEAR + [wide, wide],
        [(wide, BF16)],
        *ordered(mixed, OUTGOING),
        *ordered(other, OUTGOING),
        pair,
        gating,
        valid,
        gains,
        out_gains,
        chosen,
        weights,
    )
    near = swap_all(near, 0)
    half = rows * cols

    got = [None] * NEAR
    earlier = valid
    for d in INCOMING:
        got[d] = unpacked(near[d], 2, earlier)
        earlier = got[d][0]
    lefts, rights = zip(*got, strict=True)

    def incoming(micros, *jobs):
        return call(
            functools.partial(incoming_kernel, rows, width, jobs),
            micros,
            [(ch, total)] * sum(2 * len(sides) for dh, sides in jobs),
            [((2, width * ch, LANES), F32)],
            *lefts,
            *rights,
        )

    first = incoming(1.0, (1, (0,)))
    second = incoming(2.5, (1, (1,)), (0, (0, 1)))
    parts = [second[2:], [first[0], second[0], first[1], second[1]]]
    own, gating = call(
        functools.partial(own_kernel, chunk, cols),
        2.0,
        [((half, channels), F32)] * 2,
        [((2, total, channels), F32)],
        pair,
        normed,
        gates,
    )
    mixed = ordered(swap_all(parts[0], 0), SUMS_NEAR) + ordered(swap_all(parts[1], NEAR), SUMS_FAR)
    keep, send = call(sum_kernel, 1.0, [(NEAR * ch, half)] * 2, [], *mixed)
    got = swap(send, 0, 0, 1)
    out = call(
        functools.partial(last_kernel, chunk),
        1.0,
        [(half, channels)],
        [((channels, half), BF16)],
        keep,
        got,
        own,
        gating,
        out_gains,
        weights,
    )[0]
    return out.reshape(rows, cols, channels)


def solution(mesh):
    in_specs = (P(("groups", "row"), "col", None), P("groups"), P(), P(), P(), P(), P())
    out_specs = P(("groups", "row"), "col", None)
    direct = mesh.shape["row"] == 4 and mesh.shape["col"] == 4
    body = direct_body if direct else gather_body
    return jax.shard_map(body, mesh=mesh, in_specs=in_specs, out_specs=out_specs, check_vma=False)
```

```python
import functools

import jax
import jax.numpy as jnp
from jax import lax
from jax.experimental import pallas as pl
from jax.experimental.pallas import tpu as pltpu
from jax.sharding import PartitionSpec as P

EPSILON = 1e-05
LANES = 128
F32 = jnp.float32
BF16 = jnp.bfloat16


def layer_norm(values, gain_vec):
    mean_val = jnp.mean(values, axis=-1, keepdims=True)
    centered = values - mean_val
    variance = jnp.mean(centered * centered, axis=-1, keepdims=True)
    return centered * jax.lax.rsqrt(variance + EPSILON) * gain_vec


def project_side(pair_tile, pair_valid, layer_index, in_gain, proj_weights, gate_weight):
    normed = layer_norm(pair_tile.astype(F32), in_gain[layer_index]).astype(BF16)
    outputs = [
        jnp.dot(normed, proj_weights[layer_index, slot], preferred_element_type=F32)
        for slot in range(4)
    ]
    weight_mask = pair_valid[..., None]
    left_side = (jax.nn.sigmoid(outputs[1]) * outputs[0] * weight_mask).astype(BF16)
    right_side = (jax.nn.sigmoid(outputs[3]) * outputs[2] * weight_mask).astype(BF16)
    gating = jax.nn.sigmoid(jnp.dot(normed, gate_weight[layer_index], preferred_element_type=F32))
    return (left_side, right_side, gating)


def finish(pair_tile, mixed_sum, gating, layer_index, out_gain, out_weight):
    normed = layer_norm(mixed_sum, out_gain[layer_index]).astype(BF16)
    update = jnp.dot(normed, out_weight[layer_index], preferred_element_type=F32)
    return (pair_tile.astype(F32) + gating * update).astype(BF16)


def pair_mask(token_mask, tile_rows, row_begin, tile_cols, col_begin):
    valid = token_mask.astype(F32)
    row_valid = lax.dynamic_slice_in_dim(valid, row_begin, tile_rows, 0)
    col_valid = lax.dynamic_slice_in_dim(valid, col_begin, tile_cols, 0)
    return row_valid[:, None] * col_valid[None, :]


def gather_body(pair_map, token_mask, in_gain, proj_weights, gate_weight, out_gain, out_weight):
    tile_rows, tile_cols = pair_map.shape[:2]
    pair_valid = pair_mask(
        token_mask,
        tile_rows,
        lax.axis_index("row") * tile_rows,
        tile_cols,
        lax.axis_index("col") * tile_cols,
    )
    left_side, right_side, gating = project_side(
        pair_map, pair_valid, 0, in_gain, proj_weights, gate_weight
    )
    block = lax.all_gather(right_side, "row", axis=0, tiled=True)
    summed = lax.psum_scatter(
        jnp.einsum("jkc,ikc->jic", block, left_side, preferred_element_type=F32).astype(BF16),
        "col",
        scatter_dimension=0,
        tiled=True,
    ).astype(F32)
    mixed = jnp.transpose(summed, (1, 0, 2))
    after_out = finish(pair_map, mixed, gating, 0, out_gain, out_weight)
    left_side, right_side, gating = project_side(
        after_out, pair_valid, 1, in_gain, proj_weights, gate_weight
    )
    block = lax.all_gather(left_side, "col", axis=1, tiled=True)
    mixed = lax.psum_scatter(
        jnp.einsum("kic,kjc->ijc", block, right_side, preferred_element_type=F32).astype(BF16),
        "row",
        scatter_dimension=0,
        tiled=True,
    ).astype(F32)
    return finish(after_out, mixed, gating, 1, out_gain, out_weight)


NEAR = 4
INCOMING = (0, 1, 2, 3)
RIGHT_NEAR = (0, 1, 2, 3)
RIGHT_FAR = (0, 1, 2, 3)
OUTGOING = (0, 3, 2, 1)
SUMS_NEAR = (0, 3, 2, 1)
SUMS_FAR = (1, 0, 3, 2)


def ordered(values, order):
    return [values[d] for d in order]


def restored(values, order):
    return [values[order.index(d)] for d in range(NEAR)]


class Place:
    def __init__(self):
        z = lax.axis_index("row")
        col = lax.axis_index("col")
        self.z = z
        self.x = lax.div(col, 2)
        self.core = lax.rem(col, 2)
        self.half = lax.div(z, 2)
        self.group = lax.rem(z, 2) * 2 + self.x

    def channels(self, d, ch, other=False, compact=False, absolute=False):
        core = 1 - self.core if other else self.core
        group = d if absolute else jnp.bitwise_xor(self.group, d)
        begin = group * ch if compact else group * (2 * ch) + core * ch
        return pl.ds(pl.multiple_of(begin, ch), ch)


def lane_of(rows):
    return lax.broadcasted_iota(jnp.int32, (rows, LANES), 1)


def take_piece(value, index, width, lane):
    tile, offset = divmod(index * width, LANES)
    part = value[:, tile * LANES : (tile + 1) * LANES]
    if offset:
        part = pltpu.roll(part, LANES - offset, 1)
    if offset + width > LANES:
        after = value[:, (tile + 1) * LANES : (tile + 2) * LANES]
        part = jnp.where(lane < LANES - offset, part, pltpu.roll(after, LANES - offset, 1))
    return jnp.where(lane < width, part, jnp.zeros_like(part))


def join_pieces(piece, count, width, tile, lane):
    low = tile * LANES
    out = None
    for index in range(low // width, min(count, -(-(low + LANES) // width))):
        shift = index * width - low
        part, begin = piece(index)
        if (shift - begin) % LANES:
            part = pltpu.roll(part, (shift - begin) % LANES, 1)
        out = part if out is None else jnp.where(lane >= shift, part, out)
    return out


def norm_rows(values, gain_col, valid=None):
    mean_val = jnp.mean(values, axis=0, keepdims=True)
    centered = values - mean_val
    variance = jnp.mean(centered * centered, axis=0, keepdims=True)
    scale = lax.rsqrt(variance + EPSILON)
    if valid is not None:
        scale = scale * valid
    return (centered * scale * gain_col).astype(BF16)


def turned(weight):
    return weight.astype(F32).T.astype(BF16)


def halved(weight):
    return (weight.astype(F32) * 0.5).astype(BF16)


def project_chunk(normed, chosen):
    out = jnp.dot(chosen, normed, preferred_element_type=F32)
    half = out.shape[0] // 2
    return ((jnp.tanh(out[half:]) + 1.0) * out[:half]).astype(BF16)


def chunks_of(total, size):
    return [slice(begin, min(begin + size, total)) for begin in range(0, total, size)]


def prepare_kernel(
    pair_in,
    mask_in,
    proj_in,
    gate_in,
    weight_in,
    gain_in,
    out_gain_in,
    pair_ref,
    valid_ref,
    chosen_ref,
    gate_ref,
    weight_ref,
    gain_ref,
    out_gain_ref,
    mask_ref,
    proj_ref,
    gates_ref,
    weights_ref,
    gains_ref,
    out_gains_ref,
    turned_ref,
    sems,
):
    moves = [
        (mask_in, mask_ref),
        (proj_in, proj_ref),
        (gain_in, gains_ref),
        (out_gain_in, out_gains_ref),
        (gate_in, gates_ref),
        (weight_in, weights_ref),
        (pair_in, pair_ref),
    ]
    copies = [
        pltpu.make_async_copy(there, here, sems.at[i]) for i, (there, here) in enumerate(moves)
    ]
    for copy in copies:
        copy.start()
    place = Place()
    ch = chosen_ref.shape[1] // (4 * NEAR)
    total = valid_ref.shape[1]
    rows, cols = pair_ref.shape[:2]
    width = 2 * cols
    copies[0].wait()
    lane = lane_of(1)
    mask = mask_ref[...].astype(F32).astype(BF16)

    def lanes_from(begin):
        shape = (mask.shape[1], LANES)
        token = lax.broadcasted_iota(jnp.int32, shape, 0)
        lanes = lax.broadcasted_iota(jnp.int32, shape, 1)
        pick = jnp.where(token == lanes + begin, 1.0, 0.0).astype(BF16)
        return jnp.dot(mask, pick, preferred_element_type=F32)

    col_valid = lanes_from(place.x * width)
    row_valid = lanes_from(place.z * rows)
    for tile in range(total // LANES):
        valid_ref[:, tile * LANES : (tile + 1) * LANES] = join_pieces(
            lambda row: (col_valid * row_valid[:, row : row + 1], 0), rows, width, tile, lane
        )
    copies[1].wait()
    for layer in range(2):
        for slot in range(4):
            turned_ref[slot] = halved(turned(proj_ref[layer, (0, 2, 1, 3)[slot]]))
        for slot in range(4):
            for d in range(NEAR):
                begin = (slot * NEAR + d) * ch
                chosen_ref[layer, begin : begin + ch, :] = turned_ref[slot, place.channels(d, ch), :]
    copies[2].wait()
    copies[3].wait()
    for layer in range(2):
        for gains, ref in ((gains_ref, gain_ref), (out_gains_ref, out_gain_ref)):
            ref[layer] = jnp.broadcast_to(gains[layer : layer + 1, :], (LANES, LANES)).T
    copies[4].wait()
    copies[5].wait()
    gate_ref[0] = halved(turned(gates_ref[0]))
    weight_ref[0] = halved(turned(weights_ref[0]))
    gate_ref[1] = halved(gates_ref[1])
    weight_ref[1] = halved(weights_ref[1])
    copies[6].wait()


def column_of(ref, layer, lanes):
    return jnp.concatenate([ref[layer]] * (-(-lanes // LANES)), axis=1)[:, :lanes]


def chosen_rows(chosen_ref, layer, side):
    half = chosen_ref.shape[1] // 4
    values, gates = (side * half, (side + 1) * half), ((side + 2) * half, (side + 3) * half)
    return jnp.concatenate(
        [chosen_ref[layer, slice(*values), :], chosen_ref[layer, slice(*gates), :]], axis=0
    )


def first_kernel(
    chunk, own_ref, sibling_ref, valid_ref, gain_ref, chosen_ref, *rest
):
    far_refs, near_refs = rest[:NEAR], rest[NEAR : 2 * NEAR]
    turned_pair_ref, normed_ref, pair_ref = rest[2 * NEAR :]
    place = Place()
    cols = own_ref.shape[1]
    ch = far_refs[0].shape[0]
    total = valid_ref.shape[1]
    own_at = pl.multiple_of(place.core * cols, 8)
    sibling_at = pl.multiple_of((1 - place.core) * cols, 8)
    pair_ref[:, pl.ds(own_at, cols), :] = own_ref[...].astype(F32)
    pair_ref[:, pl.ds(sibling_at, cols), :] = sibling_ref[...].astype(F32)
    gain_col = column_of(gain_ref, 0, chunk)
    flat = pair_ref[...].reshape(total, LANES)
    sides = [chosen_rows(chosen_ref, 0, side) for side in range(2)]
    for lanes in chunks_of(total, chunk):
        pair = flat[lanes].T
        turned_pair_ref[:, lanes] = pair.astype(BF16)
        normed = norm_rows(pair, gain_col[:, : lanes.stop - lanes.start], valid_ref[:, lanes])
        normed_ref[:, lanes] = normed
        left, right = [project_chunk(normed, chosen) for chosen in sides]
        for d in range(NEAR):
            rows = slice(d * ch, (d + 1) * ch)
            far_refs[d][:, lanes] = right[rows]
            near_refs[d][:ch, lanes] = left[rows]
            near_refs[d][ch:, lanes] = right[rows]


def gate_rows(normed_ref, gate, gating_ref, chunk):
    for lanes in chunks_of(normed_ref.shape[1], chunk):
        gating_ref[:, lanes] = 1.0 + jnp.tanh(
            jnp.dot(gate, normed_ref[:, lanes], preferred_element_type=F32)
        )


def middle_kernel(chunk, *refs):
    mine = restored(refs[:NEAR], OUTGOING)
    other = restored(refs[NEAR : 2 * NEAR], OUTGOING)
    pair_ref, gating_ref, valid_ref, gain_ref, out_gain_ref = refs[2 * NEAR : 2 * NEAR + 5]
    chosen_ref, weight_ref = refs[2 * NEAR + 5 : 2 * NEAR + 7]
    near_refs = refs[2 * NEAR + 7 : 3 * NEAR + 7]
    after_ref, normed_ref, mixed_ref = refs[3 * NEAR + 7 :]
    place = Place()
    ch = mine[0].shape[0]
    total = valid_ref.shape[1]
    for d in range(NEAR):
        mixed_ref[place.channels(d, ch), :] = mine[d][...]
        mixed_ref[place.channels(d, ch, True), :] = other[d][...]
    weight = weight_ref[0]
    out_gain_col = column_of(out_gain_ref, 0, chunk)
    gain_col = column_of(gain_ref, 1, chunk)
    sides = [chosen_rows(chosen_ref, 1, side) for side in range(2)]
    for lanes in chunks_of(total, chunk):
        normed_out = norm_rows(
            mixed_ref[:, lanes].astype(F32), out_gain_col[:, : lanes.stop - lanes.start]
        )
        update = jnp.dot(weight, normed_out, preferred_element_type=F32)
        after = (pair_ref[:, lanes].astype(F32) + gating_ref[:, lanes] * update).astype(BF16)
        after_ref[:, lanes] = after
        normed = norm_rows(
            after.astype(F32), gain_col[:, : lanes.stop - lanes.start], valid_ref[:, lanes]
        )
        normed_ref[:, lanes] = normed
        for side in range(2):
            out = project_chunk(normed, sides[side])
            for d in range(NEAR):
                near_refs[d][side * ch : (side + 1) * ch, lanes] = out[d * ch : (d + 1) * ch]


def own_kernel(chunk, cols, after_ref, normed_ref, gate_ref, own_ref, gating_ref, rows_ref):
    place = Place()
    total = after_ref.shape[1]
    rows = total // (2 * cols)
    own_at = pl.multiple_of(place.core * cols, 8)
    for lanes in chunks_of(total, chunk):
        rows_ref[0, lanes, :] = after_ref[:, lanes].astype(F32).T
        rows_ref[1, lanes, :] = lax.dot_general(
            normed_ref[:, lanes],
            gate_ref[1],
            (((0,), (0,)), ((), ())),
            preferred_element_type=F32,
        )
    for row in range(rows):
        here = pl.ds(row * 2 * cols + own_at, cols)
        own_ref[row * cols : (row + 1) * cols, :] = rows_ref[0, here, :]
        gating_ref[row * cols : (row + 1) * cols, :] = 1.0 + jnp.tanh(rows_ref[1, here, :])


def sum_kernel(*refs):
    near = restored(refs[:NEAR], SUMS_NEAR)
    far = restored(refs[NEAR : 2 * NEAR], SUMS_FAR)
    keep_ref, send_ref = refs[2 * NEAR :]
    place = Place()
    ch = near[0].shape[0]
    half = keep_ref.shape[1]
    begin = half // LANES * LANES
    for d in range(NEAR):
        total = near[d][...].astype(F32) + far[d][:, : 2 * half].astype(F32)
        rows = place.channels(d, ch, compact=True)
        first = total[:, :half]
        second = pltpu.roll(total[:, begin:], half, 1)[:, :half]
        keep_ref[rows, :] = jnp.where(place.core == 0, first, second).astype(BF16)
        send_ref[rows, :] = jnp.where(place.core == 0, second, first).astype(BF16)


def last_kernel(chunk, keep_ref, got_ref, own_ref, gating_ref, gain_ref, weight_ref, out_ref, mixed_ref):
    place = Place()
    ch = keep_ref.shape[0] // NEAR
    for group in range(NEAR):
        rows = slice(group * ch, (group + 1) * ch)
        mixed_ref[place.channels(group, ch, absolute=True), :] = keep_ref[rows, :]
        mixed_ref[place.channels(group, ch, True, absolute=True), :] = got_ref[rows, :]
    for lanes in chunks_of(keep_ref.shape[1], chunk):
        gain_col = column_of(gain_ref, 1, lanes.stop - lanes.start)
        normed = norm_rows(mixed_ref[:, lanes].astype(F32), gain_col)
        update = lax.dot_general(
            normed, weight_ref[1], (((0,), (0,)), ((), ())), preferred_element_type=F32
        )
        out_ref[lanes, :] = (own_ref[lanes, :] + gating_ref[lanes, :] * update).astype(BF16)


def unpack(value, ref, begin, rows, width, lane):
    ch = value.shape[0]
    for row in range(rows):
        ref[pl.ds(begin + row * ch, ch), :] = take_piece(value, row, width, lane).astype(F32)


def pack(ref, begin, out_ref, rows, width, lane):
    ch = out_ref.shape[0]
    for tile in range(rows * width // LANES):
        out_ref[:, tile * LANES : (tile + 1) * LANES] = join_pieces(
            lambda row: (ref[pl.ds(begin + row * ch, ch), :].astype(BF16), 0), rows, width, tile, lane
        )


def pack_halves(ref, begin, out_ref, rows, cols, lane):
    ch = out_ref.shape[0]
    for tile in range(out_ref.shape[1] // LANES):
        lanes = slice(tile * LANES, (tile + 1) * LANES)
        if tile * LANES >= 2 * rows * cols:
            out_ref[:, lanes] = jnp.zeros((ch, LANES), BF16)
            continue

        def piece(index):
            part = ref[pl.ds(begin + (index % rows) * ch, ch), :].astype(BF16)
            return part, index // rows * cols

        out_ref[:, lanes] = join_pieces(piece, 2 * rows, cols, tile, lane)


def channel_of(blocks, c, ch):
    parts = []
    for column in blocks:
        rows = [ref[pl.ds(c, ref.shape[0] // ch, stride=ch), :] for ref in column]
        parts.append(jnp.concatenate(rows, axis=0))
    return jnp.concatenate(parts, axis=1).astype(BF16)


def widen(part):
    return jnp.pad(part, ((0, 0), (0, LANES - part.shape[1])))


def outgoing_multiply(left_ref, right, mixed_ref, ch):
    for c in range(ch):
        left = channel_of([[left_ref.at[0]], [left_ref.at[1]]], c, ch)
        part = lax.dot_general(
            left, channel_of(right, c, ch), (((1,), (1,)), ((), ())), preferred_element_type=F32
        )
        mixed_ref[pl.ds(c, left.shape[0], stride=ch), :] = widen(part)


def outgoing_near_kernel(rows, width, *refs):
    near = restored(refs[:NEAR], RIGHT_NEAR)
    normed_ref, gate_ref = refs[NEAR : NEAR + 2]
    gating_ref, left_ref, *outs = refs[NEAR + 2 : NEAR + 6]
    right_ref, mixed_ref = refs[NEAR + 6 :]
    gate_rows(normed_ref, gate_ref[0], gating_ref, 13 * LANES)
    place = Place()
    ch = outs[0].shape[0]
    lane = lane_of(ch)
    for d in range(NEAR):
        dl, dx = divmod(d, 2)
        value = near[d][...]
        unpack(value[:ch], left_ref.at[dx], dl * rows * ch, rows, width, lane)
        low = jnp.bitwise_xor(lax.rem(place.z, 2), dl)
        begin = pl.multiple_of(low * (rows * ch), 16)
        unpack(value[ch:], right_ref.at[dx], begin, rows, width, lane)
    outgoing_multiply(left_ref, [[right_ref.at[0]], [right_ref.at[1]]], mixed_ref, ch)
    for dl in range(2):
        pack(mixed_ref, dl * rows * ch, outs[dl], rows, width, lane)


def unpack_kernel(rows, width, value_ref, earlier_ref, *outs):
    ch = value_ref.shape[0] // len(outs)
    lane = lane_of(ch)
    for side, out_ref in enumerate(outs):
        unpack(value_ref[side * ch : (side + 1) * ch, :], out_ref, 0, rows, width, lane)


def outgoing_far_kernel(rows, width, *refs):
    far, left_ref, done = refs[:NEAR], refs[NEAR], refs[NEAR + 1 : NEAR + 3]
    outs = refs[NEAR + 3 : 2 * NEAR + 3]
    mixed_ref = refs[2 * NEAR + 3]
    place = Place()
    ch = outs[0].shape[0]
    lane = lane_of(ch)
    low = lax.rem(place.z, 2)
    for flip in range(2):

        @pl.when(low == flip)
        def _(flip=flip):
            right = [[far[2 * (zl ^ flip) + dx] for zl in range(2)] for dx in range(2)]
            outgoing_multiply(left_ref, right, mixed_ref, ch)

    same = jnp.bitwise_xor(place.half, place.x)
    for dx in range(2):

        @pl.when(same == dx)
        def _(dx=dx):
            for dl in range(2):
                outs[2 * dl + dx][...] = done[dl][...]
                pack(mixed_ref, dl * rows * ch, outs[2 * dl + 1 - dx], rows, width, lane)


def incoming_kernel(rows, width, jobs, *refs):
    lefts, rights, outs, mixed_ref = refs[:NEAR], refs[NEAR : 2 * NEAR], refs[2 * NEAR : -1], refs[-1]
    place = Place()
    ch = outs[0].shape[0]
    lane = lane_of(ch)
    for dh, sides in jobs:
        wanted = jnp.bitwise_xor(jnp.bitwise_xor(place.half, dh), place.x)
        right = [[rights[dx], rights[2 + dx]] for dx in sides]
        for dx in range(2):

            @pl.when(wanted == dx)
            def _(dx=dx, right=right, sides=sides):
                for c in range(ch):
                    part = lax.dot_general(
                        channel_of([[lefts[dx], lefts[2 + dx]]], c, ch),
                        channel_of(right, c, ch),
                        (((0,), (0,)), ((), ())),
                        preferred_element_type=F32,
                    )
                    for side in range(len(sides)):
                        mixed_ref[side, pl.ds(c, width, stride=ch), :] = part[
                            :width, side * LANES : (side + 1) * LANES
                        ]

        for dl in range(2):
            low = jnp.bitwise_xor(lax.rem(place.z, 2), dl)
            begin = pl.multiple_of(low * (rows * ch), 16)
            for side in range(len(sides)):
                out_ref, *outs = outs
                pack_halves(mixed_ref.at[side], begin, out_ref, rows, width // 2, lane)


def call(kernel, micros, outs, scratch, *args, space=pltpu.VMEM):
    outs = [(out, BF16) if isinstance(out[0], int) else out for out in outs]
    if space is pltpu.HBM:
        args = [pltpu.with_memory_space_constraint(arg, space) for arg in args]
    return pl.pallas_call(
        kernel,
        out_shape=[jax.ShapeDtypeStruct(shape, dtype) for shape, dtype in outs],
        in_specs=[pl.BlockSpec(memory_space=space) for _ in args],
        out_specs=[pl.BlockSpec(memory_space=pltpu.VMEM) for _ in outs],
        scratch_shapes=[
            entry if not isinstance(entry, tuple) else pltpu.VMEM(*entry) for entry in scratch
        ],
        compiler_params=pltpu.CompilerParams(vmem_limit_bytes=24 * 2**20),
        cost_estimate=pl.CostEstimate(
            flops=int(micros * 1.1e9), bytes_accessed=0, transcendentals=0
        ),
    )(*args)


def direct_body(pair_map, token_mask, in_gain, proj_weights, gate_weight, out_gain, out_weight):
    n_row, n_col = lax.axis_size("row"), lax.axis_size("col")
    rows, cols, channels = pair_map.shape
    width = 2 * cols
    total = rows * width
    ch = channels // (2 * NEAR)
    chunk = 25 * LANES

    def swap(value, dz, dx, core=0):
        flip = dz * n_col + dx * 2 + core
        pairs = [(i, i ^ flip) for i in range(n_row * n_col)]
        return lax.ppermute(value, ("row", "col"), pairs)

    def swap_all(values, offset):
        return [
            swap(value, *divmod(d + offset, 2)) if d + offset else value
            for d, value in enumerate(values)
        ]

    sibling = swap(pair_map, 0, 0, 1)
    wide = (channels, total)
    square = (channels, channels)
    mask = token_mask.reshape(1, -1)
    own, valid, chosen, gates, weights, gains, out_gains = call(
        prepare_kernel,
        1.5,
        [
            pair_map.shape,
            ((1, total), F32),
            (2, 4 * NEAR * ch, channels),
            (2, *square),
            (2, *square),
            ((2, *square), F32),
            ((2, *square), F32),
        ],
        [
            (mask.shape, mask.dtype),
            (proj_weights.shape, BF16),
            (gate_weight.shape, BF16),
            (out_weight.shape, BF16),
            (in_gain.shape, F32),
            (out_gain.shape, F32),
            ((4, *square), BF16),
            pltpu.SemaphoreType.DMA((7,)),
        ],
        pair_map,
        mask,
        proj_weights,
        gate_weight,
        out_weight,
        in_gain,
        out_gain,
        space=pltpu.HBM,
    )
    out = call(
        functools.partial(first_kernel, chunk),
        1.4,
        [(ch, total)] * NEAR + [(2 * ch, total)] * NEAR + [wide, wide],
        [((rows, width, channels), F32)],
        own,
        sibling,
        valid,
        gains,
        chosen,
    )
    right, near, (pair, normed) = out[:NEAR], out[NEAR : 2 * NEAR], out[2 * NEAR :]
    far = swap_all(right, NEAR)
    near = swap_all(near, 0)
    tall = 2 * rows
    side = ((tall * ch, LANES), F32)
    sides = ((2, tall * ch, LANES), F32)
    gating, left, *mixed = call(
        functools.partial(outgoing_near_kernel, rows, width),
        2.0,
        [(wide, F32), sides] + [(ch, total)] * 2,
        [sides, side],
        *ordered(near, RIGHT_NEAR),
        normed,
        gates,
    )
    block = ((rows * ch, LANES), F32)

    def unpacked(value, operands, earlier):
        return call(
            functools.partial(unpack_kernel, rows, width), 0.2, [block] * operands, [], value, earlier
        )

    blocks = []
    earlier = gating
    for value in far:
        blocks.append(unpacked(value, 1, earlier)[0])
        earlier = blocks[-1]
    mixed = call(
        functools.partial(outgoing_far_kernel, rows, width),
        1.0,
        [(ch, total)] * NEAR,
        [side],
        *blocks,
        left,
        *mixed,
    )
    mixed = swap_all(mixed, 0)
    other = [swap(part, 0, 0, 1) for part in mixed]

    *near, pair, normed = call(
        functools.partial(middle_kernel, 13 * LANES),
        2.3,
        [(2 * ch, total)] * NEAR + [wide, wide],
        [(wide, BF16)],
        *ordered(mixed, OUTGOING),
        *ordered(other, OUTGOING),
        pair,
        gating,
        valid,
        gains,
        out_gains,
        chosen,
        weights,
    )
    near = swap_all(near, 0)
    half = rows * cols

    got = [None] * NEAR
    earlier = valid
    for d in INCOMING:
        got[d] = unpacked(near[d], 2, earlier)
        earlier = got[d][0]
    lefts, rights = zip(*got, strict=True)

    def incoming(micros, *jobs):
        return call(
            functools.partial(incoming_kernel, rows, width, jobs),
            micros,
            [(ch, total)] * sum(2 * len(sides) for dh, sides in jobs),
            [((2, width * ch, LANES), F32)],
            *lefts,
            *rights,
        )

    first = incoming(1.0, (1, (0,)))
    second = incoming(2.5, (1, (1,)), (0, (0, 1)))
    parts = [second[2:], [first[0], second[0], first[1], second[1]]]
    own, gating = call(
        functools.partial(own_kernel, chunk, cols),
        2.0,
        [((half, channels), F32)] * 2,
        [((2, total, channels), F32)],
        pair,
        normed,
        gates,
    )
    mixed = ordered(swap_all(parts[0], 0), SUMS_NEAR) + ordered(swap_all(parts[1], NEAR), SUMS_FAR)
    keep, send = call(sum_kernel, 1.0, [(NEAR * ch, half)] * 2, [], *mixed)
    got = swap(send, 0, 0, 1)
    out = call(
        functools.partial(last_kernel, chunk),
        1.0,
        [(half, channels)],
        [((channels, half), BF16)],
        keep,
        got,
        own,
        gating,
        out_gains,
        weights,
    )[0]
    return out.reshape(rows, cols, channels)


def solution(mesh):
    in_specs = (P(("groups", "row"), "col", None), P("groups"), P(), P(), P(), P(), P())
    out_specs = P(("groups", "row"), "col", None)
    direct = mesh.shape["row"] == 4 and mesh.shape["col"] == 4
    body = direct_body if direct else gather_body
    return jax.shard_map(body, mesh=mesh, in_specs=in_specs, out_specs=out_specs, check_vma=False)
```
